128 devices in a mesh: dp: 8 (over x_hi, z), tensor: 16 (over x_lo, y, core).
Axes of the slice: x: 4 (x_hi: 2, x_lo: 2; x = x_hi * 2 + x_lo), y: 4, z: 4, core: 2. Of those that a mesh axis runs over, the one named last changes fastest.
Arguments:
- ckpt_values: bfloat16 [2048, 18432], P(('dp', 'tensor')), may hold values from -6 to 6
- ckpt_scales: bfloat16 [2048, 144], P(('dp', 'tensor')), may hold values from 0.25 to 4
- norm_gain: float32 [18432], replicated, may hold values from 0.5 to 1.5
- pre_act: bfloat16 [2048, 36864], P('dp', 'tensor'), may hold values from -6 to 6
- act_grad: bfloat16 [2048, 36864], P('dp', 'tensor'), may hold values from -0.09375 to 0.09375
Outputs:
- weight_grad: bfloat16 [18432, 36864], P('dp', 'tensor')
The draws below stay inside these ranges and needn't reach their ends.
All inputs are finite; a program needn't handle non-finite values.
Results may differ from the reference program's by a relative error of at most 0.0057.
Values may be sent and summed in bfloat16 or wider, within the bound.
A program may use at most 128 MiB of HBM per device.

```python
import math
import jax
import jax.numpy as jnp
from jax import lax

D = 18432
FF = 36864
QB = 128
TOKENS = 2048


def shard_levels(key, extent, pieces, least, top_value):
    level = 1.0
    for axis_at, parts in pieces:
        draws = jax.random.uniform(jax.random.fold_in(jax.random.fold_in(key, 6), axis_at), (parts,), jnp.float32, least / len(pieces), top_value / len(pieces))
        level = level * jnp.repeat(jnp.exp(draws), extent[axis_at] // parts).reshape((-1,) + (1,) * (len(extent) - 1 - axis_at))
    return level


def noise(own_key, shape, width, bound, split=(), dtype=jnp.bfloat16):
    level = shard_levels(own_key, shape, split, -0.22, 0.18) if split else 1.0
    array = jax.random.normal(own_key, shape, jnp.float32) * width * level
    return jnp.minimum(jnp.maximum(array, -bound), bound).astype(dtype)


def setup_inputs(seed: int = 0) -> dict:
    streams_of = jax.random.split(jax.random.key(seed), 6)
    return {
        "ckpt_values": noise(streams_of[0], (TOKENS, D), 1.0, 6.0, ((0, 128),)),
        "ckpt_scales": jnp.clip(jnp.exp(math.log(4.0) - 2.7725887 * jax.random.uniform(streams_of[1], (TOKENS, D // QB), jnp.float32) ** shard_levels(streams_of[1], (TOKENS, D // QB), ((0, 128),), -0.2, 0.2)), 0.25, 4.0).astype(jnp.bfloat16),
        "norm_gain": jnp.clip(1.0 + 0.1 * jax.random.normal(streams_of[2], (D,), jnp.float32), 0.5, 1.5),
        "pre_act": noise(streams_of[3], (TOKENS, FF), 1.0, 6.0, ((0, 8), (1, 16))),
        "act_grad": noise(streams_of[4], (TOKENS, FF), (2 * TOKENS) ** -0.5, 0.09375, ((0, 8), (1, 16))),
    }


def normalize(values, scales, gain):
    count = values.shape[0]
    inputs = values.astype(jnp.float32).reshape(count, D // QB, QB) * scales.astype(jnp.float32)[:, :, None]
    inputs = inputs.reshape(count, D)
    inverse = lax.rsqrt(lax.optimization_barrier(jnp.mean(inputs * inputs, axis=1, keepdims=True)) + 1e-05)
    return (inputs * inverse * gain).astype(jnp.bfloat16)

def reference(ckpt_values, ckpt_scales, norm_gain, pre_act, act_grad):
    normed = normalize(ckpt_values, ckpt_scales, norm_gain)
    pre_grad = (act_grad.astype(jnp.float32) * 2.0 * jnp.maximum(pre_act.astype(jnp.float32), 0.0)).astype(jnp.bfloat16)
    total = lax.dot_general(normed, pre_grad, (((0,), (0,)), ((), ())), preferred_element_type=jnp.float32)
    return total.astype(jnp.bfloat16)
```

```python
import functools

import jax
import jax.numpy as jnp
from jax import lax
from jax.experimental import pallas as pl
from jax.experimental.pallas import tpu as pltpu
from jax.sharding import PartitionSpec as P

MESH = pl.DeviceIdType.MESH
QB = 128
REPLICAS = 8
GROUP = 16
ROWS = 16
FEATURES = 2304
COLUMNS = 2304
WIDTH = 18432
HALF = 128
CHUNK = 64
MB = 768

SLOT = {(0, 0): 0, (0, -1): 1, (0, 1): 2, (1, 0): 3, (0, 2): 4, (1, -1): 5, (1, 1): 6, (1, 2): 7}
FAR = ((0, -1), (0, 1), (1, 0), (0, 2), (1, -1), (1, 1), (1, 2))
CONTRACT_FIRST = (((0,), (0,)), ((), ()))
COPIES = 64


def gather_kernel(
    values_hbm, scales_hbm, gain_hbm, pre_hbm, act_hbm,
    total, last_normed, last_grads,
    normed, grads, values, scales, gain, pre, act, scaled, own, send_sems, recv_sems, local_sems,
):
    dp, tensor = lax.axis_index("dp"), lax.axis_index("tensor")
    h, z = dp // 4, dp % 4
    xl, y, core = tensor // 8, (tensor // 2) % 4, tensor % 2

    def replica(dh, dz):
        return (h + dh) % 2 * 4 + (z + dz + 4) % 4

    def member(dx, dy, dc):
        return (xl + dx) % 2 * 8 + (y + dy + 4) % 4 * 2 + (core + dc) % 2

    def peer(dh=0, dz=0, dx=0, dy=0, dc=0):
        return replica(dh, dz), member(dx, dy, dc)

    started = []

    def send(src, dst, device):
        at = len(started)
        copy = pltpu.make_async_remote_copy(
            src_ref=src, dst_ref=dst, send_sem=send_sems.at[at], recv_sem=recv_sems.at[at],
            device_id=device, device_id_type=MESH,
        )
        copy.start()
        started.append(copy)
        return copy

    def load(src, dst, at):
        copy = pltpu.make_async_copy(src, dst, local_sems.at[at])
        copy.start()
        return copy

    def chunk(ref, c):
        return ref.at[c // 2, pl.ds(c % 2 * CHUNK, CHUNK)]

    pieces = {}
    for c in (0, 2):
        rows = pl.ds(c * CHUNK, CHUNK)
        pieces[c] = (load(pre_hbm.at[rows], pre.at[rows], 2 * c), load(act_hbm.at[rows], act.at[rows], 2 * c + 1))
    tokens = (load(values_hbm, values, 8), load(scales_hbm, scales, 9), load(gain_hbm, gain, 10))
    for c in (1, 3):
        rows = pl.ds(c * CHUNK, CHUNK)
        pieces[c] = (load(pre_hbm.at[rows], pre.at[rows], 2 * c), load(act_hbm.at[rows], act.at[rows], 2 * c + 1))

    friends = [peer(dh, dz) for dh, dz in FAR]
    friends += [peer(dx=1), peer(dy=1), peer(dy=-1), peer(dc=1)]
    barrier = pltpu.get_barrier_semaphore()
    for friend in friends:
        pl.semaphore_signal(barrier, inc=1, device_id=friend, device_id_type=MESH)

    def make_grad(c):
        for piece in pieces[c]:
            piece.wait()
        rows = pl.ds(c * CHUNK, CHUNK)
        product = act[rows].astype(jnp.float32) * 2.0 * jnp.maximum(pre[rows].astype(jnp.float32), 0.0)
        grads[0, c // 2, c % 2 * CHUNK : (c % 2 + 1) * CHUNK] = product.astype(jnp.bfloat16)

    def grad_send(slot, c, to_slot, **where):
        to = last_grads if to_slot == 7 else grads.at[to_slot]
        return send(chunk(grads.at[slot], c), chunk(to, c), peer(**where))

    up, down, over = {}, {}, {}

    def send_up(c):
        up[c] = grad_send(0, c, 1, dz=1)

    def send_down(c):
        down[c] = grad_send(0, c, 2, dz=-1)

    def send_over(c):
        over[c] = grad_send(0, c, 3, dh=1)

    make_grad(0)
    pl.semaphore_wait(barrier, len(friends))
    send_up(0)
    send_over(0)
    make_grad(2)
    send_down(2)

    for copy in tokens:
        copy.wait()
    squares = jnp.zeros((ROWS, QB), jnp.float32)
    for b in range(WIDTH // QB):
        at = slice(b * QB, (b + 1) * QB)
        block = values[:, at].astype(jnp.float32) * scales[:, b : b + 1].astype(jnp.float32)
        scaled[:, at] = block
        squares = squares + block * block
    mean = jnp.sum(squares, axis=1, keepdims=True) * (1.0 / WIDTH)
    inverse = lax.rsqrt(mean + 1e-05)
    for d in range(REPLICAS):
        at = slice(d * FEATURES, (d + 1) * FEATURES)
        own[d] = (scaled[:, at] * inverse * gain[:, at]).astype(jnp.bfloat16)

    def tokens_of(dx, dy, dc=0, slots=slice(None)):
        at = pl.multiple_of((y + dy + 4) % 4 * 32 + (core + dc) % 2 * 16, 16)
        return normed.at[slots, (xl + dx) % 2, pl.ds(at, ROWS)]

    def pair_of(dy, slots=slice(None)):
        at = pl.multiple_of((y + dy + 4) % 4 * 32 + core * 16, 16)
        return normed.at[slots, :, pl.ds(at, ROWS)]

    kept = load(own.at[dp], tokens_of(0, 0).at[0], 11)
    spread = []
    for dh, dz in FAR:
        spread.append(send(own.at[replica(dh, dz)], tokens_of(0, 0).at[SLOT[(dh, dz if dz == 2 else -dz)]], peer(dh, dz)))

    make_grad(1)
    make_grad(3)
    send_up(1)
    send_down(3)
    send_over(2)
    send_up(2)
    send_down(0)
    send_up(3)
    send_down(1)

    kept.wait()
    for copy in spread:
        copy.wait_recv()

    def same(ref, **where):
        return send(ref, ref, peer(**where))

    mine = tokens_of(0, 0)
    cross = same(mine, dx=1)
    mine_up, mine_down = same(mine, dy=1), same(mine, dy=-1)
    swap = [same(mine, dc=1)]
    send_over(1)
    send_over(3)

    up[0].wait_recv()
    f2_up = [grad_send(1, 0, 4, dz=1)]
    x2 = [grad_send(1, 0, 5, dh=1)]
    down[2].wait_recv()
    f2_down = [grad_send(2, 2, 4, dz=-1)]
    x2 += [grad_send(2, 2, 6, dh=1)]
    up[1].wait_recv()
    f2_up += [grad_send(1, 1, 4, dz=1)]
    down[3].wait_recv()
    f2_down += [grad_send(2, 3, 4, dz=-1)]

    cross.wait_recv()
    theirs = tokens_of(1, 0)
    theirs_up, theirs_down = same(theirs, dy=1), same(theirs, dy=-1)
    swap += [same(theirs, dc=1)]

    over[0].wait_recv()
    f3 = [grad_send(3, 0, 6, dz=-1)]
    over[2].wait_recv()
    f3 += [grad_send(3, 2, 5, dz=1)]

    mine_up.wait_recv()
    low, high = slice(0, 4), slice(4, 8)
    at_low, at_high = tokens_of(0, -1, slots=low), tokens_of(0, 1, slots=high)
    n2 = [same(at_low, dy=1)]
    mine_down.wait_recv()
    n2 += [same(at_high, dy=-1)]

    over[1].wait_recv()
    f3 += [grad_send(3, 1, 5, dz=1), grad_send(3, 1, 6, dz=-1)]
    over[3].wait_recv()
    f3 += [grad_send(3, 3, 5, dz=1), grad_send(3, 3, 6, dz=-1)]

    def accumulate(left, right, first=False):
        def step(m, carry):
            out_rows = pl.ds(pl.multiple_of(m * MB, MB), MB)
            part = lax.dot_general(
                left(out_rows), right(), CONTRACT_FIRST, preferred_element_type=jnp.float32
            )
            if first:
                total[out_rows, :] = part
            else:
                total[out_rows, :] += part
            return carry

        lax.fori_loop(0, FEATURES // MB, step, 0)

    def near(dy, first=False):
        at = pl.ds(pl.multiple_of((y + dy + 4) % 4 * 32, 32), 32)
        accumulate(
            lambda rows: normed[0:4, :, at, rows].reshape(256, MB),
            lambda: grads[0:4, :, at, :].reshape(256, COLUMNS),
            first,
        )

    def whole(slot):
        accumulate(
            lambda rows: normed[slot, :, :, rows].reshape(256, MB),
            lambda: grads[slot].reshape(256, COLUMNS),
        )

    up[2].wait_recv()
    up[3].wait_recv()
    down[0].wait_recv()
    down[1].wait_recv()
    swap[0].wait_recv()
    swap[1].wait_recv()
    near(0, first=True)

    f2_up[0].wait_recv()
    f2_down[0].wait_recv()
    f2_up[1].wait_recv()
    f4 = [grad_send(4, 1, 7, dh=1)]
    f2_down[1].wait_recv()
    f4 += [grad_send(4, 3, 7, dh=1)]

    theirs_up.wait_recv()
    n2 += [same(tokens_of(1, -1, slots=low), dy=1)]
    theirs_down.wait_recv()
    n2 += [same(tokens_of(1, 1, slots=high), dy=-1)]
    pair_low, pair_high = pair_of(-1), pair_of(1)
    swap += [same(pair_low, dc=1), same(pair_high, dc=1)]

    x2[0].wait_recv()
    f5 = [grad_send(5, 0, 7, dz=1)]
    x2[1].wait_recv()
    f5 += [grad_send(6, 2, 7, dz=-1)]

    swap[2].wait_recv()
    near(-1)
    swap[3].wait_recv()
    near(1)
    for copy in n2:
        copy.wait_recv()
    swap += [same(pair_of(2), dc=1)]
    swap[4].wait_recv()
    handed = load(normed.at[7], last_normed, 12)
    near(2)
    whole(4)
    for copy in f3:
        copy.wait_recv()
    whole(5)
    whole(6)
    handed.wait()
    for copy in f4 + f5:
        copy.wait_recv()
    for copy in started:
        copy.wait_send()


def finish_kernel(total, normed, grads, out_hbm, stage, sems):
    def store(m):
        return pltpu.make_async_copy(stage.at[m % 2], out_hbm.at[pl.ds(m * 256, 256)], sems.at[m % 2])

    steps = FEATURES // 256
    for m in range(steps):
        rows = slice(m * 256, (m + 1) * 256)
        part = lax.dot_general(
            normed[:, :, rows].reshape(256, 256), grads[...].reshape(256, COLUMNS),
            CONTRACT_FIRST, preferred_element_type=jnp.float32,
        )
        if m >= 2:
            store(m - 2).wait()
        stage[m % 2] = (total[rows, :] + part).astype(jnp.bfloat16)
        store(m).start()
    store(steps - 2).wait()
    store(steps - 1).wait()


def on_device(ckpt_values, ckpt_scales, norm_gain, pre_act, act_grad):
    any_space = pl.BlockSpec(memory_space=pl.ANY)
    vmem = pl.BlockSpec(memory_space=pltpu.VMEM)
    block = (REPLICAS, 2, HALF, COLUMNS)
    total, last_normed, last_grads = pl.pallas_call(
        gather_kernel,
        out_shape=(
            pltpu.VMEM((FEATURES, COLUMNS), jnp.float32),
            pltpu.VMEM(block[1:], jnp.bfloat16),
            pltpu.VMEM(block[1:], jnp.bfloat16),
        ),
        in_specs=[any_space] * 5,
        out_specs=(vmem, vmem, vmem),
        scratch_shapes=[
            pltpu.VMEM(block, jnp.bfloat16),
            pltpu.VMEM((REPLICAS - 1,) + block[1:], jnp.bfloat16),
            pltpu.VMEM((ROWS, WIDTH), jnp.bfloat16),
            pltpu.VMEM((ROWS, WIDTH // QB), jnp.bfloat16),
            pltpu.VMEM((1, WIDTH), jnp.float32),
            pltpu.VMEM((2 * HALF, COLUMNS), jnp.bfloat16),
            pltpu.VMEM((2 * HALF, COLUMNS), jnp.bfloat16),
            pltpu.VMEM((ROWS, WIDTH), jnp.float32),
            pltpu.VMEM((REPLICAS, ROWS, FEATURES), jnp.bfloat16),
            pltpu.SemaphoreType.DMA((COPIES,)),
            pltpu.SemaphoreType.DMA((COPIES,)),
            pltpu.SemaphoreType.DMA((13,)),
        ],
        compiler_params=pltpu.CompilerParams(
            collective_id=0, has_side_effects=True, vmem_limit_bytes=38 << 20
        ),
        name="gather_and_multiply",
    )(ckpt_values, ckpt_scales, norm_gain.reshape(1, WIDTH), pre_act, act_grad)
    return pl.pallas_call(
        finish_kernel,
        out_shape=jax.ShapeDtypeStruct((FEATURES, COLUMNS), jnp.bfloat16),
        in_specs=[vmem, vmem, vmem],
        out_specs=any_space,
        scratch_shapes=[pltpu.VMEM((2, 256, COLUMNS), jnp.bfloat16), pltpu.SemaphoreType.DMA((2,))],
        compiler_params=pltpu.CompilerParams(vmem_limit_bytes=8 << 20),
        name="add_last_replica",
    )(total, last_normed, last_grads)


def solution(mesh):
    in_specs = (
        P(("dp", "tensor"), None),
        P(("dp", "tensor"), None),
        P(),
        P("dp", "tensor"),
        P("dp", "tensor"),
    )
    return jax.shard_map(
        on_device, mesh=mesh, in_specs=in_specs, out_specs=P("dp", "tensor"), check_vma=False
    )
```

```python
import functools

import jax
import jax.numpy as jnp
from jax import lax
from jax.experimental import pallas as pl
from jax.experimental.pallas import tpu as pltpu
from jax.sharding import PartitionSpec as P

MESH = pl.DeviceIdType.MESH
QB = 128
REPLICAS = 8
GROUP = 16
ROWS = 16
FEATURES = 2304
COLUMNS = 2304
WIDTH = 18432
HALF = 128
CHUNK = 64
MB = 768

SLOT = {(0, 0): 0, (0, -1): 1, (0, 1): 2, (1, 0): 3, (0, 2): 4, (1, -1): 5, (1, 1): 6, (1, 2): 7}
EXCHANGED = (3, 5, 6, 7)
FAR = ((0, -1), (0, 1), (1, 0), (0, 2), (1, -1), (1, 1), (1, 2))
CONTRACT_FIRST = (((0,), (0,)), ((), ()))
COPIES = 80
SIDE = 1152
MOVED = 16


def gather_kernel(
    values_hbm, scales_hbm, gain_hbm, pre_hbm, act_hbm,
    left_done, right_total, last_normed, last_grads,
    left_total, normed, grads, values, scales, gain, pre, act, scaled, own, send_sems, recv_sems, local_sems,
):
    dp, tensor = lax.axis_index("dp"), lax.axis_index("tensor")
    h, z = dp // 4, dp % 4
    xl, y, core = tensor // 8, (tensor // 2) % 4, tensor % 2

    def peer(dh=0, dz=0, dx=0, dy=0, dc=0):
        return (
            (h + dh) % 2 * 4 + (z + dz + 4) % 4,
            (xl + dx) % 2 * 8 + (y + dy + 4) % 4 * 2 + (core + dc) % 2,
        )

    started = []

    def send(src, dst, device):
        at = len(started)
        copy = pltpu.make_async_remote_copy(
            src_ref=src, dst_ref=dst, send_sem=send_sems.at[at], recv_sem=recv_sems.at[at],
            device_id=device, device_id_type=MESH,
        )
        copy.start()
        started.append(copy)
        return copy

    def arrived(*copies):
        for copy in copies:
            copy.wait_recv()

    def load(src, dst, at):
        copy = pltpu.make_async_copy(src, dst, local_sems.at[at])
        copy.start()
        return copy

    def offset(c):
        return (c + y // 2) % 2 * CHUNK

    def load_chunk(c):
        rows = pl.ds(pl.multiple_of(c // 2 * HALF + offset(c), CHUNK), CHUNK)
        return load(pre_hbm.at[rows], pre.at[c], 2 * c), load(act_hbm.at[rows], act.at[c], 2 * c + 1)

    loads = {c: load_chunk(c) for c in (0, 2)}
    tokens = (load(values_hbm, values, 8), load(scales_hbm, scales, 9), load(gain_hbm, gain, 10))
    loads.update({c: load_chunk(c) for c in (1, 3)})

    friends = [peer(dh, dz, dx=dh) for dh, dz in FAR]
    friends += [peer(dh=1), peer(dx=1), peer(dy=1), peer(dy=-1), peer(dc=1)]
    barrier = pltpu.get_barrier_semaphore()
    for friend in friends:
        pl.semaphore_signal(barrier, inc=1, device_id=friend, device_id_type=MESH)

    def make_grad(c, first=0, count=CHUNK):
        rows = slice(first, first + count)
        product = act[c, rows].astype(jnp.float32) * 2.0 * jnp.maximum(pre[c, rows].astype(jnp.float32), 0.0)
        to = pl.ds(pl.multiple_of(offset(c) + first, 32), count)
        grads[0, c // 2, to] = product.astype(jnp.bfloat16)

    def chunk(slot, c, first, count, columns):
        ref = last_grads if slot == 7 else grads.at[slot]
        half = 1 - c // 2 if slot in EXCHANGED else c // 2
        return ref.at[half, pl.ds(pl.multiple_of(offset(c) + first, 16), count), columns]

    def pass_on(slot, c, to_slot, first=0, count=CHUNK, columns=slice(0, COLUMNS), **where):
        return send(chunk(slot, c, first, count, columns), chunk(to_slot, c, first, count, columns), peer(**where))

    def ready(c):
        for copy in loads[c]:
            copy.wait()

    ready(0)
    make_grad(0, 0, 32)
    pl.semaphore_wait(barrier, len(friends))
    up = {0: [pass_on(0, 0, 1, 0, 32, dz=1)]}
    over = {0: [pass_on(0, 0, 3, 0, 32, dh=1)]}
    ready(2)
    make_grad(2, 0, 32)
    down = {2: [pass_on(0, 2, 2, 0, 32, dz=-1)]}

    for copy in tokens:
        copy.wait()
    squares = jnp.zeros((ROWS, QB), jnp.float32)
    for b in range(WIDTH // QB):
        at = slice(b * QB, (b + 1) * QB)
        block = values[:, at].astype(jnp.float32) * scales[:, b : b + 1].astype(jnp.float32)
        scaled[:, at] = block
        squares = squares + block * block
    mean = jnp.sum(squares, axis=1, keepdims=True) * (1.0 / WIDTH)
    inverse = lax.rsqrt(mean + 1e-05)
    for d in range(REPLICAS):
        at = slice(d * FEATURES, (d + 1) * FEATURES)
        own[d] = (scaled[:, at] * inverse * gain[:, at]).astype(jnp.bfloat16)

    def place(dx=0, dy=0, slots=slice(0, 8)):
        at = pl.multiple_of((y + dy + 4) % 4 * 32 + core * 16, 16)
        return normed.at[slots, (xl + dx) % 2, pl.ds(at, ROWS)]

    def pair_of(dy):
        at = pl.multiple_of((y + dy + 4) % 4 * 32 + core * 16, 16)
        return normed.at[:, :, pl.ds(at, ROWS)]

    kept = load(own.at[dp], place().at[0], 11)
    spread = []
    for dh, dz in FAR:
        slot = SLOT[(dh, dz if dz == 2 else -dz)]
        to, place_in_group = peer(dh, dz, dx=dh)
        spread.append(send(own.at[to], place(dx=dh).at[slot], (to, place_in_group)))

    make_grad(0, 32, 32)
    up[0] += [pass_on(0, 0, 1, 32, 32, dz=1)]
    over[0] += [pass_on(0, 0, 3, 32, 32, dh=1)]
    make_grad(2, 32, 32)
    down[2] += [pass_on(0, 2, 2, 32, 32, dz=-1)]
    ready(1)
    make_grad(1)
    up[1] = [pass_on(0, 1, 1, dz=1)]
    ready(3)
    make_grad(3)
    down[3] = [pass_on(0, 3, 2, dz=-1)]
    up[2] = [pass_on(0, 2, 1, dz=1)]
    down[0] = [pass_on(0, 0, 2, dz=-1)]
    up[3] = [pass_on(0, 3, 1, dz=1)]
    down[1] = [pass_on(0, 1, 2, dz=-1)]

    low, high = slice(0, 4), slice(4, 8)

    def same(ref, **where):
        return send(ref, ref, peer(**where))

    kept.wait()
    arrived(*spread[:3])
    cross = [same(place(slots=low), dx=1)]
    mine_up, mine_down = [same(place(slots=low), dy=1)], [same(place(slots=low), dy=-1)]
    arrived(*spread[3:])
    cross += [same(place(slots=high), dx=1)]
    mine_up += [same(place(slots=high), dy=1)]
    mine_down += [same(place(slots=high), dy=-1)]
    swap = [same(place(), dc=1)]
    over[2] = [pass_on(0, 2, 3, dh=1)]
    over[1] = [pass_on(0, 1, 3, dh=1)]
    over[3] = [pass_on(0, 3, 3, dh=1)]

    arrived(*up[0])
    far = [pass_on(1, 0, 4, dz=1)]
    side_up = [pass_on(1, 0, 5, dh=1)]
    arrived(*down[2])
    far += [pass_on(2, 2, 4, dz=-1)]
    side_down = [pass_on(2, 2, 6, dh=1)]
    arrived(*over[0])
    side_down += [pass_on(3, 0, 6, dz=-1)]
    arrived(mine_up[0])
    mine_on = [same(place(dy=-1, slots=low), dy=1)]
    arrived(*up[1])
    far_up = pass_on(1, 1, 4, dz=1)
    side_up += [pass_on(1, 1, 5, 0, MOVED, dh=1)]
    arrived(*down[3])
    far_down = pass_on(2, 3, 4, dz=-1)
    side_down += [pass_on(2, 3, 6, 0, MOVED, dh=1)]
    arrived(cross[0])
    theirs_up, theirs_down = [same(place(dx=1, slots=low), dy=1)], [same(place(dx=1, slots=low), dy=-1)]
    arrived(mine_down[1])
    mine_on += [same(place(dy=1, slots=high), dy=-1)]
    arrived(cross[1])
    theirs_up += [same(place(dx=1, slots=high), dy=1)]
    theirs_down += [same(place(dx=1, slots=high), dy=-1)]
    swap += [same(place(dx=1), dc=1)]
    arrived(*over[2])
    side_up += [pass_on(3, 2, 5, dz=1)]

    def accumulate(left, right, first=False):
        def step(m, carry):
            out_rows = pl.ds(pl.multiple_of(m * MB, MB), MB)
            part = lax.dot_general(
                left(out_rows), right(), CONTRACT_FIRST, preferred_element_type=jnp.float32
            )
            if first:
                left_total[out_rows, :] = part[:, :SIDE]
                right_total[out_rows, :] = part[:, SIDE:]
            else:
                left_total[out_rows, :] += part[:, :SIDE]
                right_total[out_rows, :] += part[:, SIDE:]
            return carry

        lax.fori_loop(0, FEATURES // MB, step, 0)

    def near(dy, first=False):
        at = pl.ds(pl.multiple_of((y + dy + 4) % 4 * 32, 32), 32)
        accumulate(
            lambda rows: normed[0:4, :, at, rows].reshape(256, MB),
            lambda: grads[0:4, :, at, :].reshape(256, COLUMNS),
            first,
        )

    def whole(slot):
        accumulate(
            lambda rows: normed[slot, :, :, rows].reshape(256, MB),
            lambda: grads[slot].reshape(256, COLUMNS),
        )

    def beside(c):
        at = pl.ds(pl.multiple_of(offset(c), CHUNK), CHUNK)
        accumulate(
            lambda rows: normed[5:7, :, at, rows].reshape(256, MB),
            lambda: grads[5:7, :, at, :].reshape(256, COLUMNS),
        )

    arrived(*up[2], *down[0], swap[0], swap[1])
    near(0, first=True)

    arrived(theirs_up[0])
    theirs_on = [same(place(dx=1, dy=-1, slots=low), dy=1)]
    arrived(theirs_down[1])
    theirs_on += [same(place(dx=1, dy=1, slots=high), dy=-1)]
    arrived(*over[1])
    side_up += [pass_on(3, 1, 5, MOVED, CHUNK - MOVED, dz=1)]
    side_down += [pass_on(3, 1, 6, dz=-1)]
    arrived(mine_up[1], theirs_up[1])
    swap += [same(pair_of(-1), dc=1)]
    arrived(mine_down[0], theirs_down[0])
    swap += [same(pair_of(1), dc=1)]
    arrived(far_up)
    left, right = slice(0, SIDE), slice(SIDE, COLUMNS)
    arrived(*over[3])
    side_up += [pass_on(3, 3, 5, dz=1)]
    side_down += [pass_on(3, 3, 6, MOVED, CHUNK - MOVED, dz=-1)]

    arrived(*up[3], *down[1], swap[2])
    near(-1)
    arrived(*mine_on, *theirs_on)
    swap += [same(pair_of(2), dc=1)]
    arrived(far_down)
    last_left = [pass_on(4, 1, 7, columns=left, dh=1), pass_on(4, 3, 7, columns=left, dh=1)]
    last_right = [pass_on(4, 1, 7, columns=right, dh=1), pass_on(4, 3, 7, columns=right, dh=1)]
    arrived(swap[3])
    near(1)
    arrived(side_up[0])
    last_left += [pass_on(5, 0, 7, columns=left, dz=1)]
    last_right += [pass_on(5, 0, 7, columns=right, dz=1)]
    arrived(swap[4])
    handed = load(normed.at[7], last_normed, 12)
    near(2)
    arrived(side_down[0])
    last_left += [pass_on(6, 2, 7, columns=left, dz=-1)]
    last_right += [pass_on(6, 2, 7, columns=right, dz=-1)]
    arrived(*far)
    whole(4)
    arrived(side_up[2], side_down[1])
    beside(0)
    arrived(side_up[1], *side_up[3:], *side_down[2:])
    beside(1)
    arrived(*last_left)

    def finish(m, carry):
        rows = pl.ds(pl.multiple_of(m * MB, MB), MB)
        part = lax.dot_general(
            normed[7, :, :, rows].reshape(256, MB), last_grads[:, :, :SIDE].reshape(256, SIDE),
            CONTRACT_FIRST, preferred_element_type=jnp.float32,
        )
        left_done[rows, :] = (left_total[rows, :] + part).astype(jnp.bfloat16)
        return carry

    lax.fori_loop(0, FEATURES // MB, finish, 0)
    handed.wait()
    arrived(*last_right)
    for copy in started:
        copy.wait_send()


def finish_kernel(left_done, right_total, normed, grads, out_hbm, stage, sems):
    steps = FEATURES // MB
    left = pltpu.make_async_copy(left_done, out_hbm.at[:, pl.ds(0, SIDE)], sems.at[steps])
    left.start()
    stores = []
    for m in range(steps):
        rows = slice(m * MB, (m + 1) * MB)
        part = lax.dot_general(
            normed[:, :, rows].reshape(256, MB), grads[:, :, SIDE:].reshape(256, SIDE),
            CONTRACT_FIRST, preferred_element_type=jnp.float32,
        )
        stage[m] = (right_total[rows, :] + part).astype(jnp.bfloat16)
        stores.append(
            pltpu.make_async_copy(stage.at[m], out_hbm.at[pl.ds(m * MB, MB), pl.ds(SIDE, SIDE)], sems.at[m])
        )
        stores[m].start()
    left.wait()
    for store in stores:
        store.wait()


def on_device(ckpt_values, ckpt_scales, norm_gain, pre_act, act_grad):
    any_space = pl.BlockSpec(memory_space=pl.ANY)
    vmem = pl.BlockSpec(memory_space=pltpu.VMEM)
    block = (REPLICAS, 2, HALF, COLUMNS)
    parts = pl.pallas_call(
        gather_kernel,
        out_shape=(
            pltpu.VMEM((FEATURES, SIDE), jnp.bfloat16),
            pltpu.VMEM((FEATURES, SIDE), jnp.float32),
            pltpu.VMEM(block[1:], jnp.bfloat16),
            pltpu.VMEM(block[1:], jnp.bfloat16),
        ),
        in_specs=[any_space] * 5,
        out_specs=(vmem,) * 4,
        scratch_shapes=[
            pltpu.VMEM((FEATURES, SIDE), jnp.float32),
            pltpu.VMEM(block, jnp.bfloat16),
            pltpu.VMEM((REPLICAS - 1,) + block[1:], jnp.bfloat16),
            pltpu.VMEM((ROWS, WIDTH), jnp.bfloat16),
            pltpu.VMEM((ROWS, WIDTH // QB), jnp.bfloat16),
            pltpu.VMEM((1, WIDTH), jnp.float32),
            pltpu.VMEM((4, CHUNK, COLUMNS), jnp.bfloat16),
            pltpu.VMEM((4, CHUNK, COLUMNS), jnp.bfloat16),
            pltpu.VMEM((ROWS, WIDTH), jnp.float32),
            pltpu.VMEM((REPLICAS, ROWS, FEATURES), jnp.bfloat16),
            pltpu.SemaphoreType.DMA((COPIES,)),
            pltpu.SemaphoreType.DMA((COPIES,)),
            pltpu.SemaphoreType.DMA((13,)),
        ],
        compiler_params=pltpu.CompilerParams(
            collective_id=0, has_side_effects=True, vmem_limit_bytes=38 << 20
        ),
        name="gather_and_multiply",
    )(ckpt_values, ckpt_scales, norm_gain.reshape(1, WIDTH), pre_act, act_grad)
    return pl.pallas_call(
        finish_kernel,
        out_shape=jax.ShapeDtypeStruct((FEATURES, COLUMNS), jnp.bfloat16),
        in_specs=[vmem] * 4,
        out_specs=any_space,
        scratch_shapes=[pltpu.VMEM((3, MB, SIDE), jnp.bfloat16), pltpu.SemaphoreType.DMA((4,))],
        compiler_params=pltpu.CompilerParams(vmem_limit_bytes=8 << 20),
        name="add_last_replica",
    )(*parts)


def solution(mesh):
    in_specs = (
        P(("dp", "tensor"), None),
        P(("dp", "tensor"), None),
        P(),
        P("dp", "tensor"),
        P("dp", "tensor"),
    )
    return jax.shard_map(
        on_device, mesh=mesh, in_specs=in_specs, out_specs=P("dp", "tensor"), check_vma=False
    )
```

```python
import functools

import jax
import jax.numpy as jnp
from jax import lax
from jax.experimental import pallas as pl
from jax.experimental.pallas import tpu as pltpu
from jax.sharding import PartitionSpec as P

MESH = pl.DeviceIdType.MESH
QB = 128
REPLICAS = 8
GROUP = 16
ROWS = 16
FEATURES = 2304
COLUMNS = 2304
WIDTH = 18432
HALF = 128
CHUNK = 64
MB = 768

SLOT = {(0, 0): 0, (0, -1): 1, (0, 1): 2, (0, 2): 3, (1, 0): 4, (1, -1): 5, (1, 1): 6, (1, 2): 7}
EXCHANGED = (4, 5, 6, 7)
FAR = ((0, -1), (0, 1), (0, 2), (1, 0), (1, -1), (1, 1), (1, 2))
CONTRACT_FIRST = (((0,), (0,)), ((), ()))
COPIES = 80
SIDE = 1152
MOVED = 16


def gather_kernel(
    values_hbm, scales_hbm, gain_hbm, pre_hbm, act_hbm,
    left_done, right_total, last_normed, last_grads,
    left_total, normed, grads, values, scales, gain, pre, act, scaled, own, send_sems, recv_sems, local_sems,
):
    dp, tensor = lax.axis_index("dp"), lax.axis_index("tensor")
    h, z = dp // 4, dp % 4
    xl, y, core = tensor // 8, (tensor // 2) % 4, tensor % 2

    def peer(dh=0, dz=0, dx=0, dy=0, dc=0):
        return (
            (h + dh) % 2 * 4 + (z + dz + 4) % 4,
            (xl + dx) % 2 * 8 + (y + dy + 4) % 4 * 2 + (core + dc) % 2,
        )

    started = []

    def send(src, dst, device):
        at = len(started)
        copy = pltpu.make_async_remote_copy(
            src_ref=src, dst_ref=dst, send_sem=send_sems.at[at], recv_sem=recv_sems.at[at],
            device_id=device, device_id_type=MESH,
        )
        copy.start()
        started.append(copy)
        return copy

    def arrived(*copies):
        for copy in copies:
            copy.wait_recv()

    def load(src, dst, at):
        copy = pltpu.make_async_copy(src, dst, local_sems.at[at])
        copy.start()
        return copy

    def offset(c):
        return (c + y // 2) % 2 * CHUNK

    def load_chunk(c):
        rows = pl.ds(pl.multiple_of(c // 2 * HALF + offset(c), CHUNK), CHUNK)
        return load(pre_hbm.at[rows], pre.at[c], 2 * c), load(act_hbm.at[rows], act.at[c], 2 * c + 1)

    tokens = (load(values_hbm, values, 8), load(scales_hbm, scales, 9), load(gain_hbm, gain, 10))
    loads = {c: load_chunk(c) for c in (0, 2, 1, 3)}

    friends = [peer(dh, dz, dx=dh) for dh, dz in FAR]
    friends += [peer(dh=1), peer(dx=1), peer(dy=1), peer(dy=-1), peer(dc=1)]
    barrier = pltpu.get_barrier_semaphore()
    for friend in friends:
        pl.semaphore_signal(barrier, inc=1, device_id=friend, device_id_type=MESH)

    def make_grad(c):
        for copy in loads[c]:
            copy.wait()
        product = act[c].astype(jnp.float32) * 2.0 * jnp.maximum(pre[c].astype(jnp.float32), 0.0)
        grads[0, c // 2, pl.ds(pl.multiple_of(offset(c), CHUNK), CHUNK)] = product.astype(jnp.bfloat16)

    def chunk(slot, c, first, count, columns):
        ref = last_grads if slot == 7 else grads.at[slot]
        half = 1 - c // 2 if slot in EXCHANGED else c // 2
        return ref.at[half, pl.ds(pl.multiple_of(offset(c) + first, 16), count), columns]

    def pass_on(slot, c, to_slot, first=0, count=CHUNK, columns=slice(0, COLUMNS), **where):
        return send(chunk(slot, c, first, count, columns), chunk(to_slot, c, first, count, columns), peer(**where))

    for copy in tokens:
        copy.wait()
    squares = jnp.zeros((ROWS, QB), jnp.float32)
    for b in range(WIDTH // QB):
        at = slice(b * QB, (b + 1) * QB)
        block = values[:, at].astype(jnp.float32) * scales[:, b : b + 1].astype(jnp.float32)
        scaled[:, at] = block
        squares = squares + block * block
    mean = jnp.sum(squares, axis=1, keepdims=True) * (1.0 / WIDTH)
    inverse = lax.rsqrt(mean + 1e-05)
    for d in range(REPLICAS):
        at = slice(d * FEATURES, (d + 1) * FEATURES)
        own[d] = (scaled[:, at] * inverse * gain[:, at]).astype(jnp.bfloat16)

    make_grad(0)
    pl.semaphore_wait(barrier, len(friends))

    def place(dx=0, dy=0, slots=slice(0, 8)):
        at = pl.multiple_of((y + dy + 4) % 4 * 32 + core * 16, 16)
        return normed.at[slots, (xl + dx) % 2, pl.ds(at, ROWS)]

    def pair_of(dy):
        at = pl.multiple_of((y + dy + 4) % 4 * 32 + core * 16, 16)
        return normed.at[:, :, pl.ds(at, ROWS)]

    kept = load(own.at[dp], place().at[0], 11)
    spread = []
    for dh, dz in FAR[4:] + FAR[:4]:
        slot = SLOT[(dh, dz if dz == 2 else -dz)]
        to, place_in_group = peer(dh, dz, dx=dh)
        spread.append(send(own.at[to], place(dx=dh).at[slot], (to, place_in_group)))

    up, down, over = {}, {}, {}
    up[0] = [pass_on(0, 0, 1, dz=1)]
    over[0] = [pass_on(0, 0, 4, dh=1)]
    make_grad(2)
    down[2] = [pass_on(0, 2, 2, dz=-1)]
    make_grad(1)
    up[1] = [pass_on(0, 1, 1, dz=1)]
    make_grad(3)
    down[3] = [pass_on(0, 3, 2, dz=-1)]
    up[2] = [pass_on(0, 2, 1, dz=1)]
    down[0] = [pass_on(0, 0, 2, dz=-1)]
    up[3] = [pass_on(0, 3, 1, dz=1)]
    down[1] = [pass_on(0, 1, 2, dz=-1)]

    low, high = slice(0, 4), slice(4, 8)

    def same(ref, **where):
        return send(ref, ref, peer(**where))

    kept.wait()
    arrived(*spread[3:6])
    cross = [same(place(slots=low), dx=1)]
    mine_up, mine_down = [same(place(slots=low), dy=1)], [same(place(slots=low), dy=-1)]
    arrived(*spread[:3], spread[6])
    cross += [same(place(slots=high), dx=1)]
    mine_up += [same(place(slots=high), dy=1)]
    mine_down += [same(place(slots=high), dy=-1)]
    swap = [same(place(), dc=1)]
    over[2] = [pass_on(0, 2, 4, dh=1)]

    far, side = {}, {}
    arrived(*up[0])
    far[0] = pass_on(1, 0, 3, dz=1)
    arrived(*down[2])
    far[2] = pass_on(2, 2, 3, dz=-1)
    arrived(*over[0])
    side["d0"] = pass_on(4, 0, 6, dz=-1)
    arrived(cross[0])
    theirs_up, theirs_down = [same(place(dx=1, slots=low), dy=1)], [same(place(dx=1, slots=low), dy=-1)]
    arrived(mine_up[0])
    mine_on = [same(place(dy=-1, slots=low), dy=1)]
    arrived(*up[1])
    far[1] = pass_on(1, 1, 3, dz=1)
    arrived(*down[3])
    far[3] = pass_on(2, 3, 3, dz=-1)
    arrived(cross[1])
    over[1] = [pass_on(0, 1, 4, dh=1)]
    over[3] = [pass_on(0, 3, 4, dh=1)]
    theirs_up += [same(place(dx=1, slots=high), dy=1)]
    theirs_down += [same(place(dx=1, slots=high), dy=-1)]
    swap += [same(place(dx=1), dc=1)]
    side["u0"] = pass_on(1, 0, 5, dh=1)
    side["d2"] = pass_on(2, 2, 6, dh=1)
    side["moved"] = pass_on(1, 1, 5, 0, MOVED, dh=1)
    side["moved_down"] = pass_on(2, 3, 6, 0, MOVED, dh=1)
    arrived(mine_down[1])
    mine_on += [same(place(dy=1, slots=high), dy=-1)]
    arrived(*over[2])
    side["u2"] = pass_on(4, 2, 5, dz=1)

    def accumulate(left, right, first=False):
        def step(m, carry):
            out_rows = pl.ds(pl.multiple_of(m * MB, MB), MB)
            part = lax.dot_general(
                left(out_rows), right(), CONTRACT_FIRST, preferred_element_type=jnp.float32
            )
            if first:
                left_total[out_rows, :] = part[:, :SIDE]
                right_total[out_rows, :] = part[:, SIDE:]
            else:
                left_total[out_rows, :] += part[:, :SIDE]
                right_total[out_rows, :] += part[:, SIDE:]
            return carry

        lax.fori_loop(0, FEATURES // MB, step, 0)

    def near(dy, first=False):
        at = pl.ds(pl.multiple_of((y + dy + 4) % 4 * 32, 32), 32)
        accumulate(
            lambda rows: jnp.concatenate(
                [normed[0:3, :, at, rows].reshape(192, MB), normed[4, :, at, rows].reshape(64, MB)]
            ),
            lambda: jnp.concatenate(
                [grads[0:3, :, at, :].reshape(192, COLUMNS), grads[4, :, at, :].reshape(64, COLUMNS)]
            ),
            first,
        )

    def whole(slot):
        accumulate(
            lambda rows: normed[slot, :, :, rows].reshape(256, MB),
            lambda: grads[slot].reshape(256, COLUMNS),
        )

    def beside(c):
        at = pl.ds(pl.multiple_of(offset(c), CHUNK), CHUNK)
        accumulate(
            lambda rows: normed[5:7, :, at, rows].reshape(256, MB),
            lambda: grads[5:7, :, at, :].reshape(256, COLUMNS),
        )

    arrived(*up[2], *down[0], swap[0], swap[1])
    near(0, first=True)

    arrived(theirs_up[0])
    theirs_on = [same(place(dx=1, dy=-1, slots=low), dy=1)]
    arrived(theirs_down[1])
    theirs_on += [same(place(dx=1, dy=1, slots=high), dy=-1)]
    arrived(mine_up[1], theirs_up[1])
    swap += [same(pair_of(-1), dc=1)]
    arrived(mine_down[0], theirs_down[0])
    swap += [same(pair_of(1), dc=1)]
    arrived(*over[1])
    side["u1"] = pass_on(4, 1, 5, MOVED, CHUNK - MOVED, dz=1)
    side["d1"] = pass_on(4, 1, 6, dz=-1)
    arrived(far[1])
    arrived(*over[3])
    side["u3"] = pass_on(4, 3, 5, dz=1)
    side["d3"] = pass_on(4, 3, 6, MOVED, CHUNK - MOVED, dz=-1)

    arrived(*up[3], *down[1], swap[2])
    near(-1)
    arrived(*mine_on, *theirs_on)
    swap += [same(pair_of(2), dc=1)]
    arrived(swap[3])
    near(1)

    left, right = slice(0, SIDE), slice(SIDE, COLUMNS)
    arrived(far[3])
    last_left = [pass_on(3, 1, 7, columns=left, dh=1), pass_on(3, 3, 7, columns=left, dh=1)]
    last_right = [pass_on(3, 1, 7, columns=right, dh=1), pass_on(3, 3, 7, columns=right, dh=1)]
    arrived(swap[4])
    handed = load(normed.at[7], last_normed, 12)
    near(2)
    arrived(side["u0"])
    last_left += [pass_on(5, 0, 7, columns=left, dz=1)]
    last_right += [pass_on(5, 0, 7, columns=right, dz=1)]
    arrived(side["d2"])
    last_left += [pass_on(6, 2, 7, columns=left, dz=-1)]
    last_right += [pass_on(6, 2, 7, columns=right, dz=-1)]
    arrived(far[0], far[2])
    whole(3)
    arrived(side["u2"], side["d0"])
    beside(0)
    arrived(side["u1"], side["d1"], side["u3"], side["d3"], side["moved"], side["moved_down"])
    beside(1)
    arrived(*last_left)

    def finish(m, carry):
        rows = pl.ds(pl.multiple_of(m * MB, MB), MB)
        part = lax.dot_general(
            normed[7, :, :, rows].reshape(256, MB), last_grads[:, :, :SIDE].reshape(256, SIDE),
            CONTRACT_FIRST, preferred_element_type=jnp.float32,
        )
        left_done[rows, :] = (left_total[rows, :] + part).astype(jnp.bfloat16)
        return carry

    lax.fori_loop(0, FEATURES // MB, finish, 0)
    handed.wait()
    arrived(*last_right)
    for copy in started:
        copy.wait_send()


def finish_kernel(left_done, right_total, normed, grads, out_hbm, stage, sems):
    steps = FEATURES // MB
    left = pltpu.make_async_copy(left_done, out_hbm.at[:, pl.ds(0, SIDE)], sems.at[steps])
    left.start()
    stores = []
    for m in range(steps):
        rows = slice(m * MB, (m + 1) * MB)
        part = lax.dot_general(
            normed[:, :, rows].reshape(256, MB), grads[:, :, SIDE:].reshape(256, SIDE),
            CONTRACT_FIRST, preferred_element_type=jnp.float32,
        )
        stage[m] = (right_total[rows, :] + part).astype(jnp.bfloat16)
        stores.append(
            pltpu.make_async_copy(stage.at[m], out_hbm.at[pl.ds(m * MB, MB), pl.ds(SIDE, SIDE)], sems.at[m])
        )
        stores[m].start()
    left.wait()
    for store in stores:
        store.wait()


def on_device(ckpt_values, ckpt_scales, norm_gain, pre_act, act_grad):
    any_space = pl.BlockSpec(memory_space=pl.ANY)
    vmem = pl.BlockSpec(memory_space=pltpu.VMEM)
    block = (REPLICAS, 2, HALF, COLUMNS)
    parts = pl.pallas_call(
        gather_kernel,
        out_shape=(
            pltpu.VMEM((FEATURES, SIDE), jnp.bfloat16),
            pltpu.VMEM((FEATURES, SIDE), jnp.float32),
            pltpu.VMEM(block[1:], jnp.bfloat16),
            pltpu.VMEM(block[1:], jnp.bfloat16),
        ),
        in_specs=[any_space] * 5,
        out_specs=(vmem,) * 4,
        scratch_shapes=[
            pltpu.VMEM((FEATURES, SIDE), jnp.float32),
            pltpu.VMEM(block, jnp.bfloat16),
            pltpu.VMEM((REPLICAS - 1,) + block[1:], jnp.bfloat16),
            pltpu.VMEM((ROWS, WIDTH), jnp.bfloat16),
            pltpu.VMEM((ROWS, WIDTH // QB), jnp.bfloat16),
            pltpu.VMEM((1, WIDTH), jnp.float32),
            pltpu.VMEM((4, CHUNK, COLUMNS), jnp.bfloat16),
            pltpu.VMEM((4, CHUNK, COLUMNS), jnp.bfloat16),
            pltpu.VMEM((ROWS, WIDTH), jnp.float32),
            pltpu.VMEM((REPLICAS, ROWS, FEATURES), jnp.bfloat16),
            pltpu.SemaphoreType.DMA((COPIES,)),
            pltpu.SemaphoreType.DMA((COPIES,)),
            pltpu.SemaphoreType.DMA((13,)),
        ],
        compiler_params=pltpu.CompilerParams(
            collective_id=0, has_side_effects=True, vmem_limit_bytes=38 << 20
        ),
        name="gather_and_multiply",
    )(ckpt_values, ckpt_scales, norm_gain.reshape(1, WIDTH), pre_act, act_grad)
    return pl.pallas_call(
        finish_kernel,
        out_shape=jax.ShapeDtypeStruct((FEATURES, COLUMNS), jnp.bfloat16),
        in_specs=[vmem] * 4,
        out_specs=any_space,
        scratch_shapes=[pltpu.VMEM((3, MB, SIDE), jnp.bfloat16), pltpu.SemaphoreType.DMA((4,))],
        compiler_params=pltpu.CompilerParams(vmem_limit_bytes=8 << 20),
        name="add_last_replica",
    )(*parts)


def solution(mesh):
    in_specs = (
        P(("dp", "tensor"), None),
        P(("dp", "tensor"), None),
        P(),
        P("dp", "tensor"),
        P("dp", "tensor"),
    )
    return jax.shard_map(
        on_device, mesh=mesh, in_specs=in_specs, out_specs=P("dp", "tensor"), check_vma=False
    )
```

```python
import math

import jax
import jax.numpy as jnp
from jax import lax
from jax.experimental import pallas as pl
from jax.experimental.pallas import tpu as pltpu
from jax.sharding import PartitionSpec as P

MESH = pl.DeviceIdType.MESH
QB = 128
REPLICAS = 8
GROUP = 16
ROWS = 16
FEATURES = 2304
COLUMNS = 2304
WIDTH = 18432
HALF = 128
CHUNK = 64
MB = 768

SLOT = {(0, 0): 0, (0, -1): 1, (0, 1): 2, (0, 2): 3, (1, 0): 4, (1, -1): 5, (1, 1): 6, (1, 2): 7}
EXCHANGED = (4, 5, 6, 7)
FAR = ((0, -1), (0, 1), (0, 2), (1, 0), (1, -1), (1, 1), (1, 2))
CONTRACT_FIRST = (((0,), (0,)), ((), ()))
WAITS = 32
SIDE = 1152
MOVED = 16


def gather_kernel(
    values_hbm, scales_hbm, gain_hbm, pre_hbm, act_hbm,
    left_done, right_total, last_normed, last_grads,
    left_total, normed, grads, values, scales, gain, pre, act, scaled, own, send_sems, recv_sems, local_sems,
):
    dp, tensor = lax.axis_index("dp"), lax.axis_index("tensor")
    h, z = dp // 4, dp % 4
    xl, y, core = tensor // 8, (tensor // 2) % 4, tensor % 2

    def peer(dh=0, dz=0, dx=0, dy=0, dc=0):
        return (
            (h + dh) % 2 * 4 + (z + dz + 4) % 4,
            (xl + dx) % 2 * 8 + (y + dy + 4) % 4 * 2 + (core + dc) % 2,
        )

    arrivals, departures, sizes = {}, {}, {}

    def units(ref):
        return math.prod(ref.shape) // (ROWS * FEATURES)

    def send(src, dst, device, key=None):
        size = units(src)
        sizes[size] = sizes.get(size, 0) + 1
        key = ("copy", len(arrivals)) if key is None else key
        group = (size, (sizes[size] - 1) // 8)
        for table, name in ((arrivals, key), (departures, group)):
            at, count, total = table.get(name, (len(table), 0, 0))
            table[name] = (at, count + 1, total + size)
        pltpu.make_async_remote_copy(
            src_ref=src, dst_ref=dst, send_sem=send_sems.at[departures[group][0]],
            recv_sem=recv_sems.at[arrivals[key][0]], device_id=device, device_id_type=MESH,
        ).start()
        return key

    def take(semaphore, total):
        amount = normed.at[0, 0, pl.ds(0, ROWS * total)] if total <= 8 else normed.at[pl.ds(0, total // 8), 0]
        assert units(amount) == total
        pltpu.make_async_copy(amount, amount, semaphore).wait()

    def arrived(*keys):
        for key in dict.fromkeys(keys):
            at, count, total = arrivals[key]
            assert keys.count(key) == count
            take(recv_sems.at[at], total)

    def load(src, dst, at):
        copy = pltpu.make_async_copy(src, dst, local_sems.at[at])
        copy.start()
        return copy

    def offset(c):
        return (c + y // 2) % 2 * CHUNK

    def load_chunk(c):
        rows = pl.ds(pl.multiple_of(c // 2 * HALF + offset(c), CHUNK), CHUNK)
        load(pre_hbm.at[rows], pre.at[c], c)
        load(act_hbm.at[rows], act.at[c], c)
        return local_sems.at[c]

    tokens = (load(values_hbm, values, 4), load(scales_hbm, scales, 7), load(gain_hbm, gain, 8))
    loads = {c: load_chunk(c) for c in (0, 2, 1, 3)}

    friends = [peer(dh, dz, dx=dh) for dh, dz in FAR]
    friends += [peer(dh=1), peer(dx=1), peer(dy=1), peer(dy=-1), peer(dc=1)]
    barrier = pltpu.get_barrier_semaphore()
    for friend in friends:
        pl.semaphore_signal(barrier, inc=1, device_id=friend, device_id_type=MESH)

    def make_grad(c):
        take(loads[c], 8)
        product = act[c].astype(jnp.float32) * 2.0 * jnp.maximum(pre[c].astype(jnp.float32), 0.0)
        grads[0, c // 2, pl.ds(pl.multiple_of(offset(c), CHUNK), CHUNK)] = product.astype(jnp.bfloat16)

    def chunk(slot, c, first, count, columns):
        ref = last_grads if slot == 7 else grads.at[slot]
        half = 1 - c // 2 if slot in EXCHANGED else c // 2
        return ref.at[half, pl.ds(pl.multiple_of(offset(c) + first, 16), count), columns]

    def pass_on(slot, c, to_slot, first=0, count=CHUNK, columns=slice(0, COLUMNS), key=None, **where):
        there = chunk(to_slot, c, first, count, columns)
        return send(chunk(slot, c, first, count, columns), there, peer(**where), key)

    for copy in tokens:
        copy.wait()
    squares = jnp.zeros((ROWS, QB), jnp.float32)
    for b in range(WIDTH // QB):
        at = slice(b * QB, (b + 1) * QB)
        block = values[:, at].astype(jnp.float32) * scales[:, b : b + 1].astype(jnp.float32)
        scaled[:, at] = block
        squares = squares + block * block
    mean = jnp.sum(squares, axis=1, keepdims=True) * (1.0 / WIDTH)
    inverse = lax.rsqrt(mean + 1e-05)
    for d in range(REPLICAS):
        at = slice(d * FEATURES, (d + 1) * FEATURES)
        own[d] = (scaled[:, at] * inverse * gain[:, at]).astype(jnp.bfloat16)

    make_grad(0)
    pl.semaphore_wait(barrier, len(friends))

    def place(dx=0, dy=0, slots=slice(0, 8)):
        at = pl.multiple_of((y + dy + 4) % 4 * 32 + core * 16, 16)
        return normed.at[slots, (xl + dx) % 2, pl.ds(at, ROWS)]

    def pair_of(dy):
        at = pl.multiple_of((y + dy + 4) % 4 * 32 + core * 16, 16)
        return normed.at[:, :, pl.ds(at, ROWS)]

    kept = load(own.at[dp], place().at[0], 5)
    spread = []
    for dh, dz in FAR[4:] + FAR[:4]:
        slot = SLOT[(dh, dz if dz == 2 else -dz)]
        to, place_in_group = peer(dh, dz, dx=dh)
        spread.append(send(own.at[to], place(dx=dh).at[slot], (to, place_in_group), ("slices", dh)))

    up, down, over = {}, {}, {}
    up[0] = [pass_on(0, 0, 1, dz=1)]
    over[0] = [pass_on(0, 0, 4, dh=1)]
    make_grad(2)
    down[2] = [pass_on(0, 2, 2, dz=-1)]
    make_grad(1)
    up[1] = [pass_on(0, 1, 1, dz=1)]
    make_grad(3)
    down[3] = [pass_on(0, 3, 2, dz=-1)]
    up[2] = [pass_on(0, 2, 1, dz=1, key="first")]
    down[0] = [pass_on(0, 0, 2, dz=-1, key="first")]
    up[3] = [pass_on(0, 3, 1, dz=1, key="second")]
    down[1] = [pass_on(0, 1, 2, dz=-1, key="second")]

    low, high = slice(0, 4), slice(4, 8)

    def same(ref, key=None, **where):
        return send(ref, ref, peer(**where), key)

    kept.wait()
    arrived(*spread[3:6])
    cross = [same(place(slots=low), dx=1)]
    mine_up, mine_down = [same(place(slots=low), dy=1)], [same(place(slots=low), dy=-1, key="above")]
    arrived(*spread[:3], spread[6])
    cross += [same(place(slots=high), dx=1)]
    mine_up += [same(place(slots=high), dy=1, key="below")]
    mine_down += [same(place(slots=high), dy=-1)]
    swap = [same(place(), dc=1, key="first")]
    over[2] = [pass_on(0, 2, 4, dh=1)]

    far, side = {}, {}
    arrived(*up[0])
    far[0] = pass_on(1, 0, 3, dz=1, key="far")
    arrived(*down[2])
    far[2] = pass_on(2, 2, 3, dz=-1, key="far")
    arrived(*over[0])
    side["d0"] = pass_on(4, 0, 6, dz=-1, key="beside0")
    arrived(cross[0])
    theirs_up = [same(place(dx=1, slots=low), dy=1)]
    theirs_down = [same(place(dx=1, slots=low), dy=-1, key="above")]
    arrived(mine_up[0])
    mine_on = [same(place(dy=-1, slots=low), dy=1, key="opposite")]
    arrived(*up[1])
    far[1] = pass_on(1, 1, 3, dz=1)
    arrived(*down[3])
    far[3] = pass_on(2, 3, 3, dz=-1)
    arrived(cross[1])
    over[1] = [pass_on(0, 1, 4, dh=1)]
    over[3] = [pass_on(0, 3, 4, dh=1)]
    theirs_up += [same(place(dx=1, slots=high), dy=1, key="below")]
    theirs_down += [same(place(dx=1, slots=high), dy=-1)]
    swap += [same(place(dx=1), dc=1, key="first")]
    side["u0"] = pass_on(1, 0, 5, dh=1)
    side["d2"] = pass_on(2, 2, 6, dh=1)
    side["moved"] = pass_on(1, 1, 5, 0, MOVED, dh=1, key="beside1")
    side["moved_down"] = pass_on(2, 3, 6, 0, MOVED, dh=1, key="beside1")
    arrived(mine_down[1])
    mine_on += [same(place(dy=1, slots=high), dy=-1, key="opposite")]
    arrived(*over[2])
    side["u2"] = pass_on(4, 2, 5, dz=1, key="beside0")

    def accumulate(left, right, first=False):
        def step(m, carry):
            out_rows = pl.ds(pl.multiple_of(m * MB, MB), MB)
            part = lax.dot_general(
                left(out_rows), right(), CONTRACT_FIRST, preferred_element_type=jnp.float32
            )
            if first:
                left_total[out_rows, :] = part[:, :SIDE]
                right_total[out_rows, :] = part[:, SIDE:]
            else:
                left_total[out_rows, :] += part[:, :SIDE]
                right_total[out_rows, :] += part[:, SIDE:]
            return carry

        lax.fori_loop(0, FEATURES // MB, step, 0)

    def near(dy, first=False):
        at = pl.ds(pl.multiple_of((y + dy + 4) % 4 * 32, 32), 32)
        accumulate(
            lambda rows: jnp.concatenate(
                [normed[0:3, :, at, rows].reshape(192, MB), normed[4, :, at, rows].reshape(64, MB)]
            ),
            lambda: jnp.concatenate(
                [grads[0:3, :, at, :].reshape(192, COLUMNS), grads[4, :, at, :].reshape(64, COLUMNS)]
            ),
            first,
        )

    def whole(slot):
        accumulate(
            lambda rows: normed[slot, :, :, rows].reshape(256, MB),
            lambda: grads[slot].reshape(256, COLUMNS),
        )

    def beside(c):
        at = pl.ds(pl.multiple_of(offset(c), CHUNK), CHUNK)
        accumulate(
            lambda rows: normed[5:7, :, at, rows].reshape(256, MB),
            lambda: grads[5:7, :, at, :].reshape(256, COLUMNS),
        )

    arrived(*up[2], *down[0], swap[0], swap[1])
    near(0, first=True)

    arrived(theirs_up[0])
    theirs_on = [same(place(dx=1, dy=-1, slots=low), dy=1, key="opposite")]
    arrived(theirs_down[1])
    theirs_on += [same(place(dx=1, dy=1, slots=high), dy=-1, key="opposite")]
    arrived(mine_up[1], theirs_up[1])
    swap += [same(pair_of(-1), dc=1, key="second")]
    arrived(mine_down[0], theirs_down[0])
    swap += [same(pair_of(1), dc=1)]
    arrived(*over[1])
    side["u1"] = pass_on(4, 1, 5, MOVED, CHUNK - MOVED, dz=1, key="beside1")
    side["d1"] = pass_on(4, 1, 6, dz=-1, key="beside1")
    arrived(far[1])
    arrived(*over[3])
    side["u3"] = pass_on(4, 3, 5, dz=1, key="beside1")
    side["d3"] = pass_on(4, 3, 6, MOVED, CHUNK - MOVED, dz=-1, key="beside1")

    arrived(*up[3], *down[1], swap[2])
    near(-1)
    arrived(*mine_on, *theirs_on)
    swap += [same(pair_of(2), dc=1)]
    arrived(swap[3])
    near(1)

    left, right = slice(0, SIDE), slice(SIDE, COLUMNS)
    arrived(far[3])
    last_left = [pass_on(3, 1, 7, columns=left, dh=1, key="left"), pass_on(3, 3, 7, columns=left, dh=1, key="left")]
    last_right = [pass_on(3, 1, 7, columns=right, dh=1, key="right"), pass_on(3, 3, 7, columns=right, dh=1, key="right")]
    arrived(swap[4])
    handed = load(normed.at[7], last_normed, 6)
    near(2)
    arrived(side["u0"])
    last_left += [pass_on(5, 0, 7, columns=left, dz=1, key="left")]
    last_right += [pass_on(5, 0, 7, columns=right, dz=1, key="right")]
    arrived(side["d2"])
    last_left += [pass_on(6, 2, 7, columns=left, dz=-1, key="left")]
    last_right += [pass_on(6, 2, 7, columns=right, dz=-1, key="right")]
    arrived(far[0], far[2])
    whole(3)
    arrived(side["u2"], side["d0"])
    beside(0)
    arrived(side["u1"], side["d1"], side["u3"], side["d3"], side["moved"], side["moved_down"])
    beside(1)
    arrived(*last_left)

    def finish(m, carry):
        rows = pl.ds(pl.multiple_of(m * MB, MB), MB)
        part = lax.dot_general(
            normed[7, :, :, rows].reshape(256, MB), last_grads[:, :, :SIDE].reshape(256, SIDE),
            CONTRACT_FIRST, preferred_element_type=jnp.float32,
        )
        left_done[rows, :] = (left_total[rows, :] + part).astype(jnp.bfloat16)
        return carry

    lax.fori_loop(0, FEATURES // MB, finish, 0)
    handed.wait()
    arrived(*last_right)
    for at, _, total in departures.values():
        take(send_sems.at[at], total)


def finish_kernel(left_done, right_total, normed, grads, out_hbm, stage, sems):
    steps = FEATURES // MB
    left = pltpu.make_async_copy(left_done, out_hbm.at[:, pl.ds(0, SIDE)], sems.at[steps])
    left.start()
    stores = []
    for m in range(steps):
        rows = slice(m * MB, (m + 1) * MB)
        part = lax.dot_general(
            normed[:, :, rows].reshape(256, MB), grads[:, :, SIDE:].reshape(256, SIDE),
            CONTRACT_FIRST, preferred_element_type=jnp.float32,
        )
        stage[m] = (right_total[rows, :] + part).astype(jnp.bfloat16)
        stores.append(
            pltpu.make_async_copy(stage.at[m], out_hbm.at[pl.ds(m * MB, MB), pl.ds(SIDE, SIDE)], sems.at[m])
        )
        stores[m].start()
    left.wait()
    for store in stores:
        store.wait()


def on_device(ckpt_values, ckpt_scales, norm_gain, pre_act, act_grad):
    any_space = pl.BlockSpec(memory_space=pl.ANY)
    vmem = pl.BlockSpec(memory_space=pltpu.VMEM)
    block = (REPLICAS, 2, HALF, COLUMNS)
    parts = pl.pallas_call(
        gather_kernel,
        out_shape=(
            pltpu.VMEM((FEATURES, SIDE), jnp.bfloat16),
            pltpu.VMEM((FEATURES, SIDE), jnp.float32),
            pltpu.VMEM(block[1:], jnp.bfloat16),
            pltpu.VMEM(block[1:], jnp.bfloat16),
        ),
        in_specs=[any_space] * 5,
        out_specs=(vmem,) * 4,
        scratch_shapes=[
            pltpu.VMEM((FEATURES, SIDE), jnp.float32),
            pltpu.VMEM(block, jnp.bfloat16),
            pltpu.VMEM((REPLICAS - 1,) + block[1:], jnp.bfloat16),
            pltpu.VMEM((ROWS, WIDTH), jnp.bfloat16),
            pltpu.VMEM((ROWS, WIDTH // QB), jnp.bfloat16),
            pltpu.VMEM((1, WIDTH), jnp.float32),
            pltpu.VMEM((4, CHUNK, COLUMNS), jnp.bfloat16),
            pltpu.VMEM((4, CHUNK, COLUMNS), jnp.bfloat16),
            pltpu.VMEM((ROWS, WIDTH), jnp.float32),
            pltpu.VMEM((REPLICAS, ROWS, FEATURES), jnp.bfloat16),
            pltpu.SemaphoreType.DMA((12,)),
            pltpu.SemaphoreType.DMA((WAITS,)),
            pltpu.SemaphoreType.DMA((9,)),
        ],
        compiler_params=pltpu.CompilerParams(
            collective_id=0, has_side_effects=True, vmem_limit_bytes=38 << 20
        ),
        name="gather_and_multiply",
    )(ckpt_values, ckpt_scales, norm_gain.reshape(1, WIDTH), pre_act, act_grad)
    return pl.pallas_call(
        finish_kernel,
        out_shape=jax.ShapeDtypeStruct((FEATURES, COLUMNS), jnp.bfloat16),
        in_specs=[vmem] * 4,
        out_specs=any_space,
        scratch_shapes=[pltpu.VMEM((3, MB, SIDE), jnp.bfloat16), pltpu.SemaphoreType.DMA((4,))],
        compiler_params=pltpu.CompilerParams(vmem_limit_bytes=8 << 20),
        name="add_last_replica",
    )(*parts)


def solution(mesh):
    in_specs = (
        P(("dp", "tensor"), None),
        P(("dp", "tensor"), None),
        P(),
        P("dp", "tensor"),
        P("dp", "tensor"),
    )
    return jax.shard_map(
        on_device, mesh=mesh, in_specs=in_specs, out_specs=P("dp", "tensor"), check_vma=False
    )
```

```python
import math

import jax
import jax.numpy as jnp
from jax import lax
from jax.experimental import pallas as pl
from jax.experimental.pallas import tpu as pltpu
from jax.sharding import PartitionSpec as P

MESH = pl.DeviceIdType.MESH
QB = 128
REPLICAS = 8
GROUP = 16
ROWS = 16
FEATURES = 2304
COLUMNS = 2304
WIDTH = 18432
HALF = 128
CHUNK = 64
MB = 768

SLOT = {(0, 0): 0, (0, -1): 1, (0, 1): 2, (0, 2): 3, (1, 0): 4, (1, -1): 5, (1, 1): 6, (1, 2): 7}
EXCHANGED = (4, 5, 6, 7)
FAR = ((0, -1), (0, 1), (0, 2), (1, 0), (1, -1), (1, 1), (1, 2))
CONTRACT_FIRST = (((0,), (0,)), ((), ()))
WAITS = 32
SIDE = 1152
MOVED = 16


def gather_kernel(
    values_hbm, scales_hbm, gain_hbm, pre_hbm, act_hbm,
    left_done, right_total, last_normed, last_grads,
    left_total, normed, grads, values, scales, gain, pre, act, scaled, own, send_sems, recv_sems, local_sems,
):
    dp, tensor = lax.axis_index("dp"), lax.axis_index("tensor")
    h, z = dp // 4, dp % 4
    xl, y, core = tensor // 8, (tensor // 2) % 4, tensor % 2

    def peer(dh=0, dz=0, dx=0, dy=0, dc=0):
        return (
            (h + dh) % 2 * 4 + (z + dz + 4) % 4,
            (xl + dx) % 2 * 8 + (y + dy + 4) % 4 * 2 + (core + dc) % 2,
        )

    arrivals, departures, sizes = {}, {}, {}

    def units(ref):
        return math.prod(ref.shape) // (ROWS * FEATURES)

    def send(src, dst, device, key=None):
        size = units(src)
        sizes[size] = sizes.get(size, 0) + 1
        key = ("copy", len(arrivals)) if key is None else key
        group = (size, (sizes[size] - 1) // 8)
        for table, name in ((arrivals, key), (departures, group)):
            at, count, total = table.get(name, (len(table), 0, 0))
            table[name] = (at, count + 1, total + size)
        pltpu.make_async_remote_copy(
            src_ref=src, dst_ref=dst, send_sem=send_sems.at[departures[group][0]],
            recv_sem=recv_sems.at[arrivals[key][0]], device_id=device, device_id_type=MESH,
        ).start()
        return key

    def take(semaphore, total):
        amount = normed.at[0, 0, pl.ds(0, ROWS * total)] if total <= 8 else normed.at[pl.ds(0, total // 8), 0]
        assert units(amount) == total
        pltpu.make_async_copy(amount, amount, semaphore).wait()

    def arrived(*keys):
        for key in dict.fromkeys(keys):
            at, count, total = arrivals[key]
            assert keys.count(key) == count
            take(recv_sems.at[at], total)

    def load(src, dst, at):
        copy = pltpu.make_async_copy(src, dst, local_sems.at[at])
        copy.start()
        return copy

    def offset(c):
        return (c + y // 2) % 2 * CHUNK

    def load_chunk(c):
        rows = pl.ds(pl.multiple_of(c // 2 * HALF + offset(c), CHUNK), CHUNK)
        load(pre_hbm.at[rows], pre.at[c], c)
        load(act_hbm.at[rows], act.at[c], c)
        return local_sems.at[c]

    tokens = (load(values_hbm, values, 4), load(scales_hbm, scales, 7), load(gain_hbm, gain, 8))

    friends = [peer(dh, dz, dx=dh) for dh, dz in FAR]
    friends += [peer(dh=1), peer(dx=1), peer(dy=1), peer(dy=-1), peer(dc=1)]
    barrier = pltpu.get_barrier_semaphore()
    for friend in friends:
        pl.semaphore_signal(barrier, inc=1, device_id=friend, device_id_type=MESH)
    loads = {c: load_chunk(c) for c in (0, 2, 1, 3)}

    def make_grad(c):
        take(loads[c], 8)
        product = act[c].astype(jnp.float32) * 2.0 * jnp.maximum(pre[c].astype(jnp.float32), 0.0)
        grads[0, c // 2, pl.ds(pl.multiple_of(offset(c), CHUNK), CHUNK)] = product.astype(jnp.bfloat16)

    def chunk(slot, c, first, count, columns):
        ref = last_grads if slot == 7 else grads.at[slot]
        half = 1 - c // 2 if slot in EXCHANGED else c // 2
        return ref.at[half, pl.ds(pl.multiple_of(offset(c) + first, 16), count), columns]

    def pass_on(slot, c, to_slot, first=0, count=CHUNK, columns=slice(0, COLUMNS), key=None, **where):
        there = chunk(to_slot, c, first, count, columns)
        return send(chunk(slot, c, first, count, columns), there, peer(**where), key)

    for copy in tokens:
        copy.wait()
    squares = jnp.zeros((ROWS, QB), jnp.float32)
    for b in range(WIDTH // QB):
        at = slice(b * QB, (b + 1) * QB)
        block = values[:, at].astype(jnp.float32) * scales[:, b : b + 1].astype(jnp.float32)
        scaled[:, at] = block
        squares = squares + block * block
    mean = jnp.sum(squares, axis=1, keepdims=True) * (1.0 / WIDTH)
    inverse = lax.rsqrt(mean + 1e-05)

    def make_slice(to):
        at = pl.ds(pl.multiple_of(to * FEATURES, QB), FEATURES)
        own[to] = (scaled[:, at] * inverse * gain[:, at]).astype(jnp.bfloat16)

    pl.semaphore_wait(barrier, len(friends))

    def place(dx=0, dy=0, slots=slice(0, 8)):
        at = pl.multiple_of((y + dy + 4) % 4 * 32 + core * 16, 16)
        return normed.at[slots, (xl + dx) % 2, pl.ds(at, ROWS)]

    def pair_of(dy):
        at = pl.multiple_of((y + dy + 4) % 4 * 32 + core * 16, 16)
        return normed.at[:, :, pl.ds(at, ROWS)]

    spread = []
    for dh, dz in FAR[4:] + FAR[:4]:
        slot = SLOT[(dh, dz if dz == 2 else -dz)]
        to, place_in_group = peer(dh, dz, dx=dh)
        make_slice(to)
        spread.append(send(own.at[to], place(dx=dh).at[slot], (to, place_in_group), ("slices", dh)))

    make_grad(0)
    make_slice(dp)
    kept = load(own.at[dp], place().at[0], 5)

    up, down, over = {}, {}, {}
    up[0] = [pass_on(0, 0, 1, dz=1)]
    over[0] = [pass_on(0, 0, 4, dh=1)]
    make_grad(2)
    down[2] = [pass_on(0, 2, 2, dz=-1)]
    make_grad(1)
    up[1] = [pass_on(0, 1, 1, dz=1)]
    make_grad(3)
    down[3] = [pass_on(0, 3, 2, dz=-1)]
    up[2] = [pass_on(0, 2, 1, dz=1, key="first")]
    down[0] = [pass_on(0, 0, 2, dz=-1, key="first")]
    up[3] = [pass_on(0, 3, 1, dz=1, key="second")]
    down[1] = [pass_on(0, 1, 2, dz=-1, key="second")]

    low, high = slice(0, 4), slice(4, 8)

    def same(ref, key=None, **where):
        return send(ref, ref, peer(**where), key)

    kept.wait()
    arrived(*spread[3:6])
    cross = [same(place(slots=low), dx=1)]
    mine_up, mine_down = [same(place(slots=low), dy=1)], [same(place(slots=low), dy=-1, key="above")]
    arrived(*spread[:3], spread[6])
    cross += [same(place(slots=high), dx=1)]
    mine_up += [same(place(slots=high), dy=1, key="below")]
    mine_down += [same(place(slots=high), dy=-1)]
    swap = [same(place(), dc=1, key="first")]
    over[2] = [pass_on(0, 2, 4, dh=1)]

    far, side = {}, {}
    arrived(*up[0])
    far[0] = pass_on(1, 0, 3, dz=1, key="far")
    arrived(*down[2])
    far[2] = pass_on(2, 2, 3, dz=-1, key="far")
    arrived(*over[0])
    side["d0"] = pass_on(4, 0, 6, dz=-1, key="beside0")
    arrived(cross[0])
    theirs_up = [same(place(dx=1, slots=low), dy=1)]
    theirs_down = [same(place(dx=1, slots=low), dy=-1, key="above")]
    arrived(mine_up[0])
    mine_on = [same(place(dy=-1, slots=low), dy=1, key="opposite")]
    arrived(*up[1])
    far[1] = pass_on(1, 1, 3, dz=1)
    arrived(*down[3])
    far[3] = pass_on(2, 3, 3, dz=-1)
    arrived(cross[1])
    over[1] = [pass_on(0, 1, 4, dh=1)]
    over[3] = [pass_on(0, 3, 4, dh=1)]
    theirs_up += [same(place(dx=1, slots=high), dy=1, key="below")]
    theirs_down += [same(place(dx=1, slots=high), dy=-1)]
    swap += [same(place(dx=1), dc=1, key="first")]
    side["u0"] = pass_on(1, 0, 5, dh=1)
    side["d2"] = pass_on(2, 2, 6, dh=1)
    side["moved"] = pass_on(1, 1, 5, 0, MOVED, dh=1, key="beside1")
    side["moved_down"] = pass_on(2, 3, 6, 0, MOVED, dh=1, key="beside1")
    arrived(mine_down[1])
    mine_on += [same(place(dy=1, slots=high), dy=-1, key="opposite")]
    arrived(*over[2])
    side["u2"] = pass_on(4, 2, 5, dz=1, key="beside0")

    def accumulate(left, right, first=False):
        def step(m, carry):
            out_rows = pl.ds(pl.multiple_of(m * MB, MB), MB)
            part = lax.dot_general(
                left(out_rows), right(), CONTRACT_FIRST, preferred_element_type=jnp.float32
            )
            if first:
                left_total[out_rows, :] = part[:, :SIDE]
                right_total[out_rows, :] = part[:, SIDE:]
            else:
                left_total[out_rows, :] += part[:, :SIDE]
                right_total[out_rows, :] += part[:, SIDE:]
            return carry

        lax.fori_loop(0, FEATURES // MB, step, 0)

    def near(dy, first=False):
        at = pl.ds(pl.multiple_of((y + dy + 4) % 4 * 32, 32), 32)
        accumulate(
            lambda rows: jnp.concatenate(
                [normed[0:3, :, at, rows].reshape(192, MB), normed[4, :, at, rows].reshape(64, MB)]
            ),
            lambda: jnp.concatenate(
                [grads[0:3, :, at, :].reshape(192, COLUMNS), grads[4, :, at, :].reshape(64, COLUMNS)]
            ),
            first,
        )

    def whole(slot):
        accumulate(
            lambda rows: normed[slot, :, :, rows].reshape(256, MB),
            lambda: grads[slot].reshape(256, COLUMNS),
        )

    def beside(c):
        at = pl.ds(pl.multiple_of(offset(c), CHUNK), CHUNK)
        accumulate(
            lambda rows: normed[5:7, :, at, rows].reshape(256, MB),
            lambda: grads[5:7, :, at, :].reshape(256, COLUMNS),
        )

    arrived(*up[2], *down[0], swap[0], swap[1])
    near(0, first=True)

    arrived(theirs_up[0])
    theirs_on = [same(place(dx=1, dy=-1, slots=low), dy=1, key="opposite")]
    arrived(theirs_down[1])
    theirs_on += [same(place(dx=1, dy=1, slots=high), dy=-1, key="opposite")]
    arrived(mine_up[1], theirs_up[1])
    swap += [same(pair_of(-1), dc=1, key="second")]
    arrived(mine_down[0], theirs_down[0])
    swap += [same(pair_of(1), dc=1)]
    arrived(*over[1])
    side["u1"] = pass_on(4, 1, 5, MOVED, CHUNK - MOVED, dz=1, key="beside1")
    side["d1"] = pass_on(4, 1, 6, dz=-1, key="beside1")
    arrived(far[1])
    arrived(*over[3])
    side["u3"] = pass_on(4, 3, 5, dz=1, key="beside1")
    side["d3"] = pass_on(4, 3, 6, MOVED, CHUNK - MOVED, dz=-1, key="beside1")

    arrived(*up[3], *down[1], swap[2])
    near(-1)
    arrived(*mine_on, *theirs_on)
    swap += [same(pair_of(2), dc=1)]
    arrived(swap[3])
    near(1)

    left, right = slice(0, SIDE), slice(SIDE, COLUMNS)
    arrived(far[3])
    last_left = [pass_on(3, 1, 7, columns=left, dh=1, key="left"), pass_on(3, 3, 7, columns=left, dh=1, key="left")]
    last_right = [pass_on(3, 1, 7, columns=right, dh=1, key="right"), pass_on(3, 3, 7, columns=right, dh=1, key="right")]
    arrived(swap[4])
    handed = load(normed.at[7], last_normed, 6)
    near(2)
    arrived(side["u0"])
    last_left += [pass_on(5, 0, 7, columns=left, dz=1, key="left")]
    last_right += [pass_on(5, 0, 7, columns=right, dz=1, key="right")]
    arrived(side["d2"])
    last_left += [pass_on(6, 2, 7, columns=left, dz=-1, key="left")]
    last_right += [pass_on(6, 2, 7, columns=right, dz=-1, key="right")]
    arrived(far[0], far[2])
    whole(3)
    arrived(side["u2"], side["d0"])
    beside(0)
    arrived(side["u1"], side["d1"], side["u3"], side["d3"], side["moved"], side["moved_down"])
    beside(1)
    arrived(*last_left)

    def finish(m, carry):
        rows = pl.ds(pl.multiple_of(m * MB, MB), MB)
        part = lax.dot_general(
            normed[7, :, :, rows].reshape(256, MB), last_grads[:, :, :SIDE].reshape(256, SIDE),
            CONTRACT_FIRST, preferred_element_type=jnp.float32,
        )
        left_done[rows, :] = (left_total[rows, :] + part).astype(jnp.bfloat16)
        return carry

    lax.fori_loop(0, FEATURES // MB, finish, 0)
    handed.wait()
    arrived(*last_right)
    for at, _, total in departures.values():
        take(send_sems.at[at], total)


def finish_kernel(left_done, right_total, normed, grads, out_hbm, stage, sems):
    steps = FEATURES // MB
    left = pltpu.make_async_copy(left_done, out_hbm.at[:, pl.ds(0, SIDE)], sems.at[steps])
    left.start()
    stores = []
    for m in range(steps):
        rows = slice(m * MB, (m + 1) * MB)
        part = lax.dot_general(
            normed[:, :, rows].reshape(256, MB), grads[:, :, SIDE:].reshape(256, SIDE),
            CONTRACT_FIRST, preferred_element_type=jnp.float32,
        )
        stage[m] = (right_total[rows, :] + part).astype(jnp.bfloat16)
        stores.append(
            pltpu.make_async_copy(stage.at[m], out_hbm.at[pl.ds(m * MB, MB), pl.ds(SIDE, SIDE)], sems.at[m])
        )
        stores[m].start()
    left.wait()
    for store in stores:
        store.wait()


def on_device(ckpt_values, ckpt_scales, norm_gain, pre_act, act_grad):
    any_space = pl.BlockSpec(memory_space=pl.ANY)
    vmem = pl.BlockSpec(memory_space=pltpu.VMEM)
    block = (REPLICAS, 2, HALF, COLUMNS)
    parts = pl.pallas_call(
        gather_kernel,
        out_shape=(
            pltpu.VMEM((FEATURES, SIDE), jnp.bfloat16),
            pltpu.VMEM((FEATURES, SIDE), jnp.float32),
            pltpu.VMEM(block[1:], jnp.bfloat16),
            pltpu.VMEM(block[1:], jnp.bfloat16),
        ),
        in_specs=[any_space] * 5,
        out_specs=(vmem,) * 4,
        scratch_shapes=[
            pltpu.VMEM((FEATURES, SIDE), jnp.float32),
            pltpu.VMEM(block, jnp.bfloat16),
            pltpu.VMEM((REPLICAS - 1,) + block[1:], jnp.bfloat16),
            pltpu.VMEM((ROWS, WIDTH), jnp.bfloat16),
            pltpu.VMEM((ROWS, WIDTH // QB), jnp.bfloat16),
            pltpu.VMEM((1, WIDTH), jnp.float32),
            pltpu.VMEM((4, CHUNK, COLUMNS), jnp.bfloat16),
            pltpu.VMEM((4, CHUNK, COLUMNS), jnp.bfloat16),
            pltpu.VMEM((ROWS, WIDTH), jnp.float32),
            pltpu.VMEM((REPLICAS, ROWS, FEATURES), jnp.bfloat16),
            pltpu.SemaphoreType.DMA((12,)),
            pltpu.SemaphoreType.DMA((WAITS,)),
            pltpu.SemaphoreType.DMA((9,)),
        ],
        compiler_params=pltpu.CompilerParams(
            collective_id=0, has_side_effects=True, vmem_limit_bytes=38 << 20
        ),
        name="gather_and_multiply",
    )(ckpt_values, ckpt_scales, norm_gain.reshape(1, WIDTH), pre_act, act_grad)
    return pl.pallas_call(
        finish_kernel,
        out_shape=jax.ShapeDtypeStruct((FEATURES, COLUMNS), jnp.bfloat16),
        in_specs=[vmem] * 4,
        out_specs=any_space,
        scratch_shapes=[pltpu.VMEM((3, MB, SIDE), jnp.bfloat16), pltpu.SemaphoreType.DMA((4,))],
        compiler_params=pltpu.CompilerParams(vmem_limit_bytes=8 << 20),
        name="add_last_replica",
    )(*parts)


def solution(mesh):
    in_specs = (
        P(("dp", "tensor"), None),
        P(("dp", "tensor"), None),
        P(),
        P("dp", "tensor"),
        P("dp", "tensor"),
    )
    return jax.shard_map(
        on_device, mesh=mesh, in_specs=in_specs, out_specs=P("dp", "tensor"), check_vma=False
    )
```

```python
import math

import jax
import jax.numpy as jnp
from jax import lax
from jax.experimental import pallas as pl
from jax.experimental.pallas import tpu as pltpu
from jax.sharding import PartitionSpec as P

MESH = pl.DeviceIdType.MESH
QB = 128
REPLICAS = 8
GROUP = 16
ROWS = 16
FEATURES = 2304
COLUMNS = 2304
WIDTH = 18432
HALF = 128
CHUNK = 64
MB = 768

SLOT = {(0, 0): 0, (0, -1): 1, (0, 1): 2, (0, 2): 3, (1, 0): 4, (1, -1): 5, (1, 1): 6, (1, 2): 7}
EXCHANGED = (4, 5, 6, 7)
FAR = ((0, -1), (0, 1), (0, 2), (1, 0), (1, -1), (1, 1), (1, 2))
CONTRACT_FIRST = (((0,), (0,)), ((), ()))
WAITS = 32
SIDE = 1152
MOVED = 16


def gather_kernel(
    values_hbm, scales_hbm, gain_hbm, pre_hbm, act_hbm,
    left_done, right_total, last_normed, last_grads,
    left_total, normed, grads, values, scales, gain, pre, act, scaled, own, send_sems, recv_sems, local_sems,
):
    dp, tensor = lax.axis_index("dp"), lax.axis_index("tensor")
    h, z = dp // 4, dp % 4
    xl, y, core = tensor // 8, (tensor // 2) % 4, tensor % 2

    def peer(dh=0, dz=0, dx=0, dy=0, dc=0):
        return (
            (h + dh) % 2 * 4 + (z + dz + 4) % 4,
            (xl + dx) % 2 * 8 + (y + dy + 4) % 4 * 2 + (core + dc) % 2,
        )

    arrivals, departures, sizes = {}, {}, {}

    def units(ref):
        return math.prod(ref.shape) // (ROWS * FEATURES)

    def send(src, dst, device, key=None):
        size = units(src)
        sizes[size] = sizes.get(size, 0) + 1
        key = ("copy", len(arrivals)) if key is None else key
        group = (size, (sizes[size] - 1) // 8)
        for table, name in ((arrivals, key), (departures, group)):
            at, count, total = table.get(name, (len(table), 0, 0))
            table[name] = (at, count + 1, total + size)
        pltpu.make_async_remote_copy(
            src_ref=src, dst_ref=dst, send_sem=send_sems.at[departures[group][0]],
            recv_sem=recv_sems.at[arrivals[key][0]], device_id=device, device_id_type=MESH,
        ).start()
        return key

    def take(semaphore, total):
        amount = normed.at[0, 0, pl.ds(0, ROWS * total)] if total <= 8 else normed.at[pl.ds(0, total // 8), 0]
        assert units(amount) == total
        pltpu.make_async_copy(amount, amount, semaphore).wait()

    def arrived(*keys):
        for key in dict.fromkeys(keys):
            at, count, total = arrivals[key]
            assert keys.count(key) == count
            take(recv_sems.at[at], total)

    def load(src, dst, at):
        copy = pltpu.make_async_copy(src, dst, local_sems.at[at])
        copy.start()
        return copy

    def offset(c):
        return (c + y // 2) % 2 * CHUNK

    def load_chunk(c):
        rows = pl.ds(pl.multiple_of(c // 2 * HALF + offset(c), CHUNK), CHUNK)
        load(pre_hbm.at[rows], pre.at[c], c)
        load(act_hbm.at[rows], act.at[c], c)
        return local_sems.at[c]

    tokens = (load(values_hbm, values, 4), load(scales_hbm, scales, 7), load(gain_hbm, gain, 8))

    friends = [peer(dh, dz, dx=dh) for dh, dz in FAR]
    friends += [peer(dh=1), peer(dx=1), peer(dy=1), peer(dy=-1), peer(dc=1)]
    barrier = pltpu.get_barrier_semaphore()
    for friend in friends:
        pl.semaphore_signal(barrier, inc=1, device_id=friend, device_id_type=MESH)
    loads = {c: load_chunk(c) for c in (0, 2, 1, 3)}

    def make_grad(c):
        take(loads[c], 8)
        product = act[c].astype(jnp.float32) * 2.0 * jnp.maximum(pre[c].astype(jnp.float32), 0.0)
        grads[0, c // 2, pl.ds(pl.multiple_of(offset(c), CHUNK), CHUNK)] = product.astype(jnp.bfloat16)

    def chunk(slot, c, first, count, columns):
        ref = last_grads if slot == 7 else grads.at[slot]
        half = 1 - c // 2 if slot in EXCHANGED else c // 2
        return ref.at[half, pl.ds(pl.multiple_of(offset(c) + first, 16), count), columns]

    def pass_on(slot, c, to_slot, first=0, count=CHUNK, columns=slice(0, COLUMNS), key=None, **where):
        there = chunk(to_slot, c, first, count, columns)
        return send(chunk(slot, c, first, count, columns), there, peer(**where), key)

    for copy in tokens:
        copy.wait()
    squares = jnp.zeros((ROWS, QB), jnp.float32)
    for b in range(WIDTH // QB):
        at = slice(b * QB, (b + 1) * QB)
        block = values[:, at].astype(jnp.float32) * scales[:, b : b + 1].astype(jnp.float32)
        scaled[:, at] = block
        squares = squares + block * block
    mean = jnp.sum(squares, axis=1, keepdims=True) * (1.0 / WIDTH)
    inverse = lax.rsqrt(mean + 1e-05)

    def make_slice(to):
        at = pl.ds(pl.multiple_of(to * FEATURES, QB), FEATURES)
        own[to] = (scaled[:, at] * inverse * gain[:, at]).astype(jnp.bfloat16)

    pl.semaphore_wait(barrier, len(friends))

    def place(dx=0, dy=0, slots=slice(0, 8)):
        at = pl.multiple_of((y + dy + 4) % 4 * 32 + core * 16, 16)
        return normed.at[slots, (xl + dx) % 2, pl.ds(at, ROWS)]

    def pair_of(dy):
        at = pl.multiple_of((y + dy + 4) % 4 * 32 + core * 16, 16)
        return normed.at[:, :, pl.ds(at, ROWS)]

    spread = []
    for dh, dz in FAR[4:] + FAR[:4]:
        slot = SLOT[(dh, dz if dz == 2 else -dz)]
        to, place_in_group = peer(dh, dz, dx=dh)
        make_slice(to)
        spread.append(send(own.at[to], place(dx=dh).at[slot], (to, place_in_group), ("slices", dh)))

    make_grad(0)

    up, down, over = {}, {}, {}
    up[0] = [pass_on(0, 0, 1, dz=1)]
    over[0] = [pass_on(0, 0, 4, dh=1)]
    make_grad(2)
    down[2] = [pass_on(0, 2, 2, dz=-1)]
    make_slice(dp)
    kept = load(own.at[dp], place().at[0], 5)
    make_grad(1)
    up[1] = [pass_on(0, 1, 1, dz=1)]
    make_grad(3)
    down[3] = [pass_on(0, 3, 2, dz=-1)]
    up[2] = [pass_on(0, 2, 1, dz=1, key="first")]
    down[0] = [pass_on(0, 0, 2, dz=-1, key="first")]
    up[3] = [pass_on(0, 3, 1, dz=1, key="second")]
    down[1] = [pass_on(0, 1, 2, dz=-1, key="second")]

    low, high = slice(0, 4), slice(4, 8)

    def same(ref, key=None, **where):
        return send(ref, ref, peer(**where), key)

    kept.wait()
    arrived(*spread[3:6])
    cross = [same(place(slots=low), dx=1)]
    mine_up, mine_down = [same(place(slots=low), dy=1)], [same(place(slots=low), dy=-1, key="above")]
    arrived(*spread[:3], spread[6])
    cross += [same(place(slots=high), dx=1)]
    mine_up += [same(place(slots=high), dy=1, key="below")]
    mine_down += [same(place(slots=high), dy=-1)]
    swap = [same(place(), dc=1, key="first")]
    over[2] = [pass_on(0, 2, 4, dh=1)]

    far, side = {}, {}
    arrived(*up[0])
    far[0] = pass_on(1, 0, 3, dz=1, key="far")
    arrived(*down[2])
    far[2] = pass_on(2, 2, 3, dz=-1, key="far")
    arrived(*over[0])
    side["d0"] = pass_on(4, 0, 6, dz=-1, key="beside0")
    arrived(cross[0])
    theirs_up = [same(place(dx=1, slots=low), dy=1)]
    theirs_down = [same(place(dx=1, slots=low), dy=-1, key="above")]
    arrived(mine_up[0])
    mine_on = [same(place(dy=-1, slots=low), dy=1, key="opposite")]
    arrived(*up[1])
    far[1] = pass_on(1, 1, 3, dz=1)
    arrived(*down[3])
    far[3] = pass_on(2, 3, 3, dz=-1)
    arrived(cross[1])
    over[1] = [pass_on(0, 1, 4, dh=1)]
    over[3] = [pass_on(0, 3, 4, dh=1)]
    theirs_up += [same(place(dx=1, slots=high), dy=1, key="below")]
    theirs_down += [same(place(dx=1, slots=high), dy=-1)]
    swap += [same(place(dx=1), dc=1, key="first")]
    side["u0"] = pass_on(1, 0, 5, dh=1)
    side["d2"] = pass_on(2, 2, 6, dh=1)
    side["moved"] = pass_on(1, 1, 5, 0, MOVED, dh=1, key="beside1")
    side["moved_down"] = pass_on(2, 3, 6, 0, MOVED, dh=1, key="beside1")
    arrived(mine_down[1])
    mine_on += [same(place(dy=1, slots=high), dy=-1, key="opposite")]
    arrived(*over[2])
    side["u2"] = pass_on(4, 2, 5, dz=1, key="beside0")

    def accumulate(left, right, first=False):
        def step(m, carry):
            out_rows = pl.ds(pl.multiple_of(m * MB, MB), MB)
            part = lax.dot_general(
                left(out_rows), right(), CONTRACT_FIRST, preferred_element_type=jnp.float32
            )
            if first:
                left_total[out_rows, :] = part[:, :SIDE]
                right_total[out_rows, :] = part[:, SIDE:]
            else:
                left_total[out_rows, :] += part[:, :SIDE]
                right_total[out_rows, :] += part[:, SIDE:]
            return carry

        lax.fori_loop(0, FEATURES // MB, step, 0)

    def near(dy, first=False):
        at = pl.ds(pl.multiple_of((y + dy + 4) % 4 * 32, 32), 32)
        accumulate(
            lambda rows: jnp.concatenate(
                [normed[0:3, :, at, rows].reshape(192, MB), normed[4, :, at, rows].reshape(64, MB)]
            ),
            lambda: jnp.concatenate(
                [grads[0:3, :, at, :].reshape(192, COLUMNS), grads[4, :, at, :].reshape(64, COLUMNS)]
            ),
            first,
        )

    def whole(slot):
        accumulate(
            lambda rows: normed[slot, :, :, rows].reshape(256, MB),
            lambda: grads[slot].reshape(256, COLUMNS),
        )

    def beside(c):
        at = pl.ds(pl.multiple_of(offset(c), CHUNK), CHUNK)
        accumulate(
            lambda rows: normed[5:7, :, at, rows].reshape(256, MB),
            lambda: grads[5:7, :, at, :].reshape(256, COLUMNS),
        )

    arrived(*up[2], *down[0], swap[0], swap[1])
    near(0, first=True)

    arrived(theirs_up[0])
    theirs_on = [same(place(dx=1, dy=-1, slots=low), dy=1, key="opposite")]
    arrived(theirs_down[1])
    theirs_on += [same(place(dx=1, dy=1, slots=high), dy=-1, key="opposite")]
    arrived(mine_up[1], theirs_up[1])
    swap += [same(pair_of(-1), dc=1, key="second")]
    arrived(mine_down[0], theirs_down[0])
    swap += [same(pair_of(1), dc=1)]
    arrived(*over[1])
    side["u1"] = pass_on(4, 1, 5, MOVED, CHUNK - MOVED, dz=1, key="beside1")
    side["d1"] = pass_on(4, 1, 6, dz=-1, key="beside1")
    arrived(far[1])
    arrived(*over[3])
    side["u3"] = pass_on(4, 3, 5, dz=1, key="beside1")
    side["d3"] = pass_on(4, 3, 6, MOVED, CHUNK - MOVED, dz=-1, key="beside1")

    arrived(*up[3], *down[1], swap[2])
    near(-1)
    arrived(*mine_on, *theirs_on)
    swap += [same(pair_of(2), dc=1)]
    arrived(swap[3])
    near(1)

    left, right = slice(0, SIDE), slice(SIDE, COLUMNS)
    arrived(far[3])
    last_left = [pass_on(3, 1, 7, columns=left, dh=1, key="left"), pass_on(3, 3, 7, columns=left, dh=1, key="left")]
    last_right = [pass_on(3, 1, 7, columns=right, dh=1, key="right"), pass_on(3, 3, 7, columns=right, dh=1, key="right")]
    arrived(swap[4])
    handed = load(normed.at[7], last_normed, 6)
    near(2)
    arrived(side["u0"])
    last_left += [pass_on(5, 0, 7, columns=left, dz=1, key="left")]
    last_right += [pass_on(5, 0, 7, columns=right, dz=1, key="right")]
    arrived(side["d2"])
    last_left += [pass_on(6, 2, 7, columns=left, dz=-1, key="left")]
    last_right += [pass_on(6, 2, 7, columns=right, dz=-1, key="right")]
    arrived(far[0], far[2])
    whole(3)
    arrived(side["u2"], side["d0"])
    beside(0)
    arrived(side["u1"], side["d1"], side["u3"], side["d3"], side["moved"], side["moved_down"])
    beside(1)
    arrived(*last_left)

    def finish(m, carry):
        rows = pl.ds(pl.multiple_of(m * MB, MB), MB)
        part = lax.dot_general(
            normed[7, :, :, rows].reshape(256, MB), last_grads[:, :, :SIDE].reshape(256, SIDE),
            CONTRACT_FIRST, preferred_element_type=jnp.float32,
        )
        left_done[rows, :] = (left_total[rows, :] + part).astype(jnp.bfloat16)
        return carry

    lax.fori_loop(0, FEATURES // MB, finish, 0)
    handed.wait()
    arrived(*last_right)
    for at, _, total in departures.values():
        take(send_sems.at[at], total)


def finish_kernel(left_done, right_total, normed, grads, out_hbm, stage, sems):
    steps = FEATURES // MB
    left = pltpu.make_async_copy(left_done, out_hbm.at[:, pl.ds(0, SIDE)], sems.at[steps])
    left.start()
    stores = []
    for m in range(steps):
        rows = slice(m * MB, (m + 1) * MB)
        part = lax.dot_general(
            normed[:, :, rows].reshape(256, MB), grads[:, :, SIDE:].reshape(256, SIDE),
            CONTRACT_FIRST, preferred_element_type=jnp.float32,
        )
        stage[m] = (right_total[rows, :] + part).astype(jnp.bfloat16)
        stores.append(
            pltpu.make_async_copy(stage.at[m], out_hbm.at[pl.ds(m * MB, MB), pl.ds(SIDE, SIDE)], sems.at[m])
        )
        stores[m].start()
    left.wait()
    for store in stores:
        store.wait()


def on_device(ckpt_values, ckpt_scales, norm_gain, pre_act, act_grad):
    any_space = pl.BlockSpec(memory_space=pl.ANY)
    vmem = pl.BlockSpec(memory_space=pltpu.VMEM)
    block = (REPLICAS, 2, HALF, COLUMNS)
    parts = pl.pallas_call(
        gather_kernel,
        out_shape=(
            pltpu.VMEM((FEATURES, SIDE), jnp.bfloat16),
            pltpu.VMEM((FEATURES, SIDE), jnp.float32),
            pltpu.VMEM(block[1:], jnp.bfloat16),
            pltpu.VMEM(block[1:], jnp.bfloat16),
        ),
        in_specs=[any_space] * 5,
        out_specs=(vmem,) * 4,
        scratch_shapes=[
            pltpu.VMEM((FEATURES, SIDE), jnp.float32),
            pltpu.VMEM(block, jnp.bfloat16),
            pltpu.VMEM((REPLICAS - 1,) + block[1:], jnp.bfloat16),
            pltpu.VMEM((ROWS, WIDTH), jnp.bfloat16),
            pltpu.VMEM((ROWS, WIDTH // QB), jnp.bfloat16),
            pltpu.VMEM((1, WIDTH), jnp.float32),
            pltpu.VMEM((4, CHUNK, COLUMNS), jnp.bfloat16),
            pltpu.VMEM((4, CHUNK, COLUMNS), jnp.bfloat16),
            pltpu.VMEM((ROWS, WIDTH), jnp.float32),
            pltpu.VMEM((REPLICAS, ROWS, FEATURES), jnp.bfloat16),
            pltpu.SemaphoreType.DMA((12,)),
            pltpu.SemaphoreType.DMA((WAITS,)),
            pltpu.SemaphoreType.DMA((9,)),
        ],
        compiler_params=pltpu.CompilerParams(
            collective_id=0, has_side_effects=True, vmem_limit_bytes=38 << 20
        ),
        name="gather_and_multiply",
    )(ckpt_values, ckpt_scales, norm_gain.reshape(1, WIDTH), pre_act, act_grad)
    return pl.pallas_call(
        finish_kernel,
        out_shape=jax.ShapeDtypeStruct((FEATURES, COLUMNS), jnp.bfloat16),
        in_specs=[vmem] * 4,
        out_specs=any_space,
        scratch_shapes=[pltpu.VMEM((3, MB, SIDE), jnp.bfloat16), pltpu.SemaphoreType.DMA((4,))],
        compiler_params=pltpu.CompilerParams(vmem_limit_bytes=8 << 20),
        name="add_last_replica",
    )(*parts)


def solution(mesh):
    in_specs = (
        P(("dp", "tensor"), None),
        P(("dp", "tensor"), None),
        P(),
        P("dp", "tensor"),
        P("dp", "tensor"),
    )
    return jax.shard_map(
        on_device, mesh=mesh, in_specs=in_specs, out_specs=P("dp", "tensor"), check_vma=False
    )
```
